32 devices in a mesh: subj: 4 (over y, x), gz: 8 (over z, core).
Axes of the slice: x: 2, y: 2, z: 4, core: 2. Of those that a mesh axis runs over, the one named last changes fastest.
Arguments:
- warped: float32 [4, 256, 64, 256], P('subj', 'gz'), may hold values from -12 to 12
Outputs:
- force: float32 [4, 3, 256, 64, 256], P('subj', None, 'gz')
- template: float32 [256, 64, 256], P('gz')
- loss: float32 [4], P('subj')
The draws below stay inside these ranges and needn't reach their ends.
All inputs are finite; a program needn't handle non-finite values.
Results may differ from the reference program's by a relative error of at most 0.0001.
Values sent between devices are 32-bit elements; how exact they have to be, the bound alone decides.
A program may use at most 128 MiB of HBM per device.

```python
import math
import jax
import jax.numpy as jnp
from jax import lax

SUBJ = 4
NY = 64
NX = 256
BOX_R = 4
GAUSS_R = 3
NZ = 256


def draw_warped(key, part):
    key_common, key_jitter = jax.random.split(jax.random.fold_in(key, 17))
    heights = jnp.arange(NZ, dtype=jnp.float32) / float(NZ)
    noise_level = (0.3 + 1.7 * heights)[None, :, None, None]
    common = jnp.clip(jax.random.normal(key_common, (1, NZ, NY, NX), jnp.float32), -4.0, 4.0)
    jitter = jnp.clip(jax.random.normal(key_jitter, (SUBJ, NZ, NY, NX), jnp.float32), -4.0, 4.0)
    return (common + noise_level * jitter).astype(jnp.float32)


def setup_inputs(seed: int = 0) -> dict:
    key_of = jax.random.split(jax.random.key(seed), 2)
    return {
        "warped": draw_warped(jax.random.fold_in(key_of[1], 71), 0),
    }


epsilon = 1e-5


def shifted_sum(padded, along, planes_out, window_span):
    running = lax.slice_in_dim(padded, 0, planes_out, axis=along)
    for offset in range(1, window_span):
        running = running + lax.slice_in_dim(padded, offset, offset + planes_out, axis=along)
    return running


def window_mean(volume):
    window_span = 2 * BOX_R + 1
    planes_out = volume.shape[0] - 2 * BOX_R
    running = shifted_sum(volume, 0, planes_out, window_span)
    running = shifted_sum(jnp.pad(running, ((0, 0), (BOX_R, BOX_R), (0, 0))), 1, volume.shape[1], window_span)
    running = shifted_sum(jnp.pad(running, ((0, 0), (0, 0), (BOX_R, BOX_R))), 2, volume.shape[2], window_span)
    return running / float(window_span ** 3)


def local_force(moving, target):
    planes_out = moving.shape[0] - 2 * BOX_R
    mean_moving = window_mean(moving)
    mean_target = window_mean(target)
    var_moving = window_mean(moving * moving) - mean_moving * mean_moving
    var_target = window_mean(target * target) - mean_target * mean_target
    cross_cov = window_mean(moving * target) - mean_moving * mean_target
    moving_core = moving[BOX_R:BOX_R + planes_out]
    target_core = target[BOX_R:BOX_R + planes_out]
    denominator = var_moving * var_target + epsilon
    similarity = cross_cov * cross_cov / denominator
    factor = 2.0 * cross_cov / denominator * ((target_core - mean_target) - cross_cov / (var_moving + epsilon) * (moving_core - mean_moving))
    slope_depth = 0.5 * (moving[BOX_R + 1:BOX_R + 1 + planes_out] - moving[BOX_R - 1:BOX_R - 1 + planes_out])
    padded_rows = jnp.pad(moving_core, ((0, 0), (1, 1), (0, 0)))
    slope_rows = 0.5 * (padded_rows[:, 2:] - padded_rows[:, :-2])
    padded_cols = jnp.pad(moving_core, ((0, 0), (0, 0), (1, 1)))
    slope_cols = 0.5 * (padded_cols[:, :, 2:] - padded_cols[:, :, :-2])
    forces = jnp.stack([factor * slope_depth, factor * slope_rows, factor * slope_cols])
    return forces, similarity


def blur_weights():
    bumps = [math.exp(-(offset * offset) / 8.0) for offset in range(-GAUSS_R, GAUSS_R + 1)]
    whole = sum(bumps)
    return [bump / whole for bump in bumps]


def weighted_sum(padded, along, planes_out, weights):
    running = weights[0] * lax.slice_in_dim(padded, 0, planes_out, axis=along)
    for offset in range(1, len(weights)):
        running = running + weights[offset] * lax.slice_in_dim(padded, offset, offset + planes_out, axis=along)
    return running


def gaussian_blur(padded):
    weights = blur_weights()
    planes_out = padded.shape[1] - 2 * GAUSS_R
    smoothed = weighted_sum(padded, 1, planes_out, weights)
    smoothed = weighted_sum(jnp.pad(smoothed, ((0, 0), (0, 0), (GAUSS_R, GAUSS_R), (0, 0))), 2, padded.shape[2], weights)
    smoothed = weighted_sum(jnp.pad(smoothed, ((0, 0), (0, 0), (0, 0), (GAUSS_R, GAUSS_R))), 3, padded.shape[3], weights)
    return smoothed


def reference(warped):
    template = jnp.sum(warped, axis=0) / SUBJ
    target_wide = jnp.pad(template, ((BOX_R, BOX_R), (0, 0), (0, 0)))
    smoothed_all = []
    losses = []
    for member in range(SUBJ):
        moving_wide = jnp.pad(warped[member], ((BOX_R, BOX_R), (0, 0), (0, 0)))
        forces, similarity = local_force(moving_wide, target_wide)
        padded = jnp.pad(forces, ((0, 0), (GAUSS_R, GAUSS_R), (0, 0), (0, 0)))
        smoothed_all.append(gaussian_blur(padded))
        losses.append(-jnp.sum(similarity) / float(NZ * NY * NX))
    return jnp.stack(smoothed_all), template, jnp.stack(losses)
```

```python
import functools
import math

import jax
import jax.numpy as jnp
import ml_dtypes
import numpy as np
from jax import lax
from jax.experimental import pallas as pl
from jax.experimental.pallas import tpu as pltpu
from jax.sharding import PartitionSpec as P

BOX_R = 4
GAUSS_R = 3
HALO = BOX_R + GAUSS_R
EPS = 1e-05
BLOCK = 8
GROUP = 4
STRIP = 16
F32 = jnp.float32
BF16 = jnp.bfloat16


def bands(rows, cols):
    bumps = np.array([math.exp(-(k * k) / 8.0) for k in range(-GAUSS_R, GAUSS_R + 1)])
    bumps = bumps / bumps.sum()

    def band(n, weights, radius):
        out = np.zeros((n, n), np.float32)
        for k in range(-radius, radius + 1):
            out += np.diag(np.full(n - abs(k), weights[k + radius], np.float32), k)
        return out

    def high_low(m):
        high = m.astype(ml_dtypes.bfloat16)
        low = (m - high.astype(np.float32)).astype(ml_dtypes.bfloat16)
        return high, low

    ones = np.ones(2 * BOX_R + 1)
    eye = np.eye(GROUP, dtype=np.float32)
    box_y = np.kron(eye, band(rows, ones, BOX_R)).astype(ml_dtypes.bfloat16)
    box_x = band(cols, ones, BOX_R).astype(ml_dtypes.bfloat16)
    gy_high, gy_low = high_low(np.kron(eye, band(rows, bumps, GAUSS_R)))
    gx_high, gx_low = high_low(band(cols, bumps, GAUSS_R))
    return (
        np.concatenate([box_y] * 3, axis=1),
        np.concatenate([box_x] * 3, axis=0),
        np.concatenate([gy_high, gy_high, gy_low], axis=1),
        np.concatenate([gx_high, gx_high, gx_low], axis=0),
        [float(b) for b in bumps[GAUSS_R:]],
    )


def split3(v):
    a = v.astype(BF16)
    r = v - a.astype(F32)
    b = r.astype(BF16)
    c = (r - b.astype(F32)).astype(BF16)
    return a, b, c


def split2(v):
    a = v.astype(BF16)
    return a, (v - a.astype(F32)).astype(BF16)


def windows(planes):
    n = BLOCK
    span = 2 * BOX_R + 1
    head = [None] * (n + 1)
    acc = planes[n - 1]
    head[n - 1] = acc
    for i in range(n - 2, -1, -1):
        acc = acc + planes[i]
        head[i] = acc
    out = []
    tail = None
    for i in range(n):
        tail = planes[n + i] if tail is None else tail + planes[n + i]
        out.append(head[i] + tail)
    assert span == n + 1
    return out


def cov_block(b, z_first, depth, planes, iw, jw, r_ref, xy, t_ref, loss, by, bx):
    rows, cols = iw.shape[1], iw.shape[2]
    base = b * BLOCK
    grows = GROUP * rows

    def strip(s, _):
        row = pl.multiple_of(s * STRIP, STRIP)
        for lane in range(0, cols, 128):
            span = BLOCK + 2 * BOX_R
            iv = [iw[base + k, pl.ds(row, STRIP), pl.ds(lane, 128)] for k in range(span)]
            jv = [jw[base + k, pl.ds(row, STRIP), pl.ds(lane, 128)] for k in range(span)]
            for v in range(5):
                if v == 0:
                    vol = iv
                elif v == 1:
                    vol = jv
                elif v == 2:
                    vol = [a * a for a in iv]
                elif v == 3:
                    vol = [a * a for a in jv]
                else:
                    vol = [a * c for a, c in zip(iv, jv)]
                for w, total in enumerate(windows(vol)):
                    g, u = w // GROUP, w % GROUP
                    for k, piece in enumerate(split3(total)):
                        at = k * grows + u * rows
                        xy[v, g, pl.ds(at + row, STRIP), pl.ds(lane, 128)] = piece
        return 0

    lax.fori_loop(0, rows // STRIP, strip, 0)

    scale = 1.0 / float((2 * BOX_R + 1) ** 3)

    def group(g, _):
        for v in range(5):
            ys = jnp.dot(by[...], xy[v, g], preferred_element_type=F32)
            xs = jnp.concatenate(split3(ys), axis=1)
            t_ref[v] = jnp.dot(xs, bx[...], preferred_element_type=F32)

        def plane(u, _):
            at = pl.multiple_of(u * rows, rows)
            c = base + g * GROUP + u
            m = [t_ref[v, pl.ds(at, rows), :] * scale for v in range(5)]
            mi, mj = m[0], m[1]
            var_i = m[2] - mi * mi
            var_j = m[3] - mj * mj
            cc = m[4] - mi * mj
            moving = iw[c + BOX_R]
            target = jw[c + BOX_R]
            q = cc / (var_i * var_j + EPS)
            z = z_first - GAUSS_R + c
            owned = jnp.logical_and(c >= GAUSS_R, c < GAUSS_R + planes)
            sim = jnp.where(owned, cc * q, 0.0)
            loss[...] += sim
            factor = q * ((target - mj) - cc / (var_i + EPS) * (moving - mi))
            inside = jnp.logical_and(z >= 0, z < depth)
            factor = jnp.where(inside, factor, 0.0)
            row_id = lax.broadcasted_iota(jnp.int32, moving.shape, 0)
            col_id = lax.broadcasted_iota(jnp.int32, moving.shape, 1)
            dz = iw[c + BOX_R + 1] - iw[c + BOX_R - 1]
            dy = jnp.where(row_id == rows - 1, 0.0, pltpu.roll(moving, rows - 1, 0)) - jnp.where(
                row_id == 0, 0.0, pltpu.roll(moving, 1, 0)
            )
            dx = jnp.where(col_id == cols - 1, 0.0, pltpu.roll(moving, cols - 1, 1)) - jnp.where(
                col_id == 0, 0.0, pltpu.roll(moving, 1, 1)
            )
            r_ref[0, c] = factor * dz
            r_ref[1, c] = factor * dy
            r_ref[2, c] = factor * dx
            return 0

        lax.fori_loop(0, GROUP, plane, 0)
        return 0

    lax.fori_loop(0, BLOCK // GROUP, group, 0)


def blur_block(b, weights, r_ref, yx, gy, gx, put):
    rows, cols = r_ref.shape[2], r_ref.shape[3]
    base = b * GROUP

    for k in range(3):

        def strip(s, _):
            row = pl.multiple_of(s * STRIP, STRIP)
            for lane in range(0, cols, 128):
                v = [
                    r_ref[k, base + j, pl.ds(row, STRIP), pl.ds(lane, 128)]
                    for j in range(GROUP + 2 * GAUSS_R)
                ]
                for u in range(GROUP):
                    mid = u + GAUSS_R
                    total = weights[0] * v[mid]
                    for o in range(1, GAUSS_R + 1):
                        total = total + weights[o] * (v[mid - o] + v[mid + o])
                    high, low = split2(total)
                    at = u * rows + row
                    yx[k, pl.ds(at, STRIP), pl.ds(lane, 128)] = high
                    yx[k, pl.ds(at, STRIP), pl.ds(cols + lane, 128)] = low
                    yx[k, pl.ds(at, STRIP), pl.ds(2 * cols + lane, 128)] = high
            return 0

        lax.fori_loop(0, rows // STRIP, strip, 0)
    for k in range(3):
        xs = jnp.dot(yx[k], gx[...], preferred_element_type=F32)
        high, low = split2(xs)
        both = jnp.concatenate([high, low, high], axis=0)
        put(k, base, jnp.dot(gy[...], both, preferred_element_type=F32))


def kernel(depth, weights, iw, jw, by, bx, gy, gx, out, loss_out, r_ref, xy, t_ref, yx, loss):
    planes, rows, cols = out.shape[1:]
    z_first = lax.axis_index("gz") * planes
    loss[...] = jnp.zeros_like(loss)
    blocks = -(-(planes + 2 * GAUSS_R) // BLOCK)

    def cov(b, _):
        cov_block(b, z_first, depth, planes, iw, jw, r_ref, xy, t_ref, loss, by, bx)
        return 0

    lax.fori_loop(0, blocks, cov, 0)

    def put(k, base, value):
        out[k, pl.ds(base, GROUP)] = jnp.reshape(value, (GROUP, rows, cols))

    def blur(b, _):
        blur_block(b, weights, r_ref, yx, gy, gx, put)
        return 0

    lax.fori_loop(0, planes // GROUP, blur, 0)
    loss_out[...] = loss[...]


def widened(array, extra):
    size = lax.axis_size("gz")
    up = [(i, i + 1) for i in range(size - 1)]
    down = [(j, i) for i, j in up]
    before = lax.ppermute(array[-HALO:], "gz", up)
    after = lax.ppermute(array[:HALO], "gz", down)
    return jnp.concatenate([before, array, after, jnp.zeros((extra,) + array.shape[1:], F32)])


def on_device(warped):
    moving = warped[0]
    planes, rows, cols = moving.shape
    depth = planes * lax.axis_size("gz")
    by, bx, gy, gx, weights = bands(rows, cols)
    cov_planes = -(-(planes + 2 * GAUSS_R) // BLOCK) * BLOCK
    extra = cov_planes + 2 * BOX_R - planes - 2 * HALO
    template = lax.psum(moving, "subj") / lax.axis_size("subj")
    iw = widened(moving, extra)
    jw = widened(template, extra)
    grows = GROUP * rows
    vmem = pl.BlockSpec(memory_space=pltpu.VMEM)
    force, sims = pl.pallas_call(
        functools.partial(kernel, depth, weights),
        out_shape=(
            jax.ShapeDtypeStruct((3, planes, rows, cols), F32),
            jax.ShapeDtypeStruct((rows, cols), F32),
        ),
        in_specs=[vmem] * 6,
        out_specs=(vmem, vmem),
        scratch_shapes=[
            pltpu.VMEM((3, cov_planes, rows, cols), F32),
            pltpu.VMEM((5, BLOCK // GROUP, 3 * grows, cols), BF16),
            pltpu.VMEM((5, grows, cols), F32),
            pltpu.VMEM((3, grows, 3 * cols), BF16),
            pltpu.VMEM((rows, cols), F32),
        ],
        compiler_params=pltpu.CompilerParams(vmem_limit_bytes=56 * 1024 * 1024),
    )(iw, jw, by, bx, gy, gx)
    loss = -lax.psum(jnp.sum(sims), "gz") / float(depth * rows * cols)
    return (force[None], template, jnp.reshape(loss, (1,)))


def solution(mesh):
    placed = (P("subj", "gz", None, None),)
    return jax.shard_map(
        on_device,
        mesh=mesh,
        in_specs=placed,
        out_specs=(P("subj", None, "gz", None, None), P("gz", None, None), P("subj")),
        check_vma=False,
    )
```

```python
import functools
import math

import jax
import jax.numpy as jnp
import ml_dtypes
import numpy as np
from jax import lax
from jax.experimental import pallas as pl
from jax.experimental.pallas import tpu as pltpu
from jax.sharding import PartitionSpec as P

BOX_R = 4
GAUSS_R = 3
EPS = 1e-05
BLOCK = 8
GROUP = 4
STRIP = 16
F32 = jnp.float32
BF16 = jnp.bfloat16
MESH = pl.DeviceIdType.MESH


def bands(rows, cols):
    bumps = np.array([math.exp(-(k * k) / 8.0) for k in range(-GAUSS_R, GAUSS_R + 1)])
    bumps = bumps / bumps.sum()

    def band(n, weights, radius):
        out = np.zeros((n, n), np.float32)
        for k in range(-radius, radius + 1):
            out += np.diag(np.full(n - abs(k), weights[k + radius], np.float32), k)
        return out

    def high_low(m):
        high = m.astype(ml_dtypes.bfloat16)
        low = (m - high.astype(np.float32)).astype(ml_dtypes.bfloat16)
        return high, low

    ones = np.ones(2 * BOX_R + 1)
    eye = np.eye(GROUP, dtype=np.float32)
    box_y = np.kron(eye, band(rows, ones, BOX_R)).astype(ml_dtypes.bfloat16)
    box_x = band(cols, ones, BOX_R).astype(ml_dtypes.bfloat16)
    gy_high, gy_low = high_low(np.kron(eye, band(rows, bumps, GAUSS_R)))
    gx_high, gx_low = high_low(band(cols, bumps, GAUSS_R))
    return (
        np.concatenate([box_y] * 3, axis=1),
        np.concatenate([box_x] * 3, axis=0),
        np.concatenate([gy_high, gy_high, gy_low], axis=1),
        np.concatenate([gx_high, gx_high, gx_low], axis=0),
        [float(b) for b in bumps[GAUSS_R:]],
    )


def split3(v):
    a = v.astype(BF16)
    r = v - a.astype(F32)
    b = r.astype(BF16)
    c = (r - b.astype(F32)).astype(BF16)
    return a, b, c


def split2(v):
    a = v.astype(BF16)
    return a, (v - a.astype(F32)).astype(BF16)


def windows(planes):
    n = BLOCK
    span = 2 * BOX_R + 1
    head = [None] * (n + 1)
    acc = planes[n - 1]
    head[n - 1] = acc
    for i in range(n - 2, -1, -1):
        acc = acc + planes[i]
        head[i] = acc
    out = []
    tail = None
    for i in range(n):
        tail = planes[n + i] if tail is None else tail + planes[n + i]
        out.append(head[i] + tail)
    assert span == n + 1
    return out


def box_block(b, first, count, iw, jw, xy, t_ref, by, bx):
    rows, cols = iw.shape[1], iw.shape[2]
    base = b * BLOCK
    grows = GROUP * rows
    span = BLOCK + 2 * BOX_R

    def strip(s, _):
        row = pl.multiple_of(s * STRIP, STRIP)
        for lane in range(0, cols, 128):
            iv = [iw[base + k, pl.ds(row, STRIP), pl.ds(lane, 128)] for k in range(span)]
            if first + count > 2:
                jv = [jw[base + k, pl.ds(row, STRIP), pl.ds(lane, 128)] for k in range(span)]
            for v in range(first, first + count):
                if v == 0:
                    vol = iv
                elif v == 1:
                    vol = [a * a for a in iv]
                elif v == 2:
                    vol = jv
                elif v == 3:
                    vol = [a * a for a in jv]
                else:
                    vol = [a * c for a, c in zip(iv, jv)]
                for w, total in enumerate(windows(vol)):
                    g, u = w // GROUP, w % GROUP
                    for k, piece in enumerate(split3(total)):
                        at = k * grows + u * rows
                        xy[v - first, g, pl.ds(at + row, STRIP), pl.ds(lane, 128)] = piece
        return 0

    lax.fori_loop(0, rows // STRIP, strip, 0)

    def group(g, _):
        at = pl.multiple_of(b * BLOCK * rows + g * grows, grows)
        for v in range(count):
            ys = jnp.dot(by[...], xy[v, g], preferred_element_type=F32)
            xs = jnp.concatenate(split3(ys), axis=1)
            t_ref[first + v, pl.ds(at, grows), :] = jnp.dot(
                xs, bx[...], preferred_element_type=F32
            )
        return 0

    lax.fori_loop(0, BLOCK // GROUP, group, 0)


def force_block(b, z_first, depth, planes, iw, jw, r_ref, t_ref, loss):
    rows, cols = iw.shape[1], iw.shape[2]
    scale = 1.0 / float((2 * BOX_R + 1) ** 3)

    def plane(u, _):
        c = b * BLOCK + u
        at = pl.multiple_of(c * rows, rows)
        m = [t_ref[v, pl.ds(at, rows), :] * scale for v in range(5)]
        mi, mj = m[0], m[2]
        var_i = m[1] - mi * mi
        var_j = m[3] - mj * mj
        cc = m[4] - mi * mj
        moving = iw[c + BOX_R]
        target = jw[c + BOX_R]
        q = cc / (var_i * var_j + EPS)
        core = c - BOX_R
        z = z_first + core
        owned = jnp.logical_and(core >= 0, core < planes)
        loss[...] += jnp.where(owned, cc * q, 0.0)
        factor = q * ((target - mj) - cc / (var_i + EPS) * (moving - mi))
        inside = jnp.logical_and(z >= 0, z < depth)
        factor = jnp.where(inside, factor, 0.0)
        row_id = lax.broadcasted_iota(jnp.int32, moving.shape, 0)
        col_id = lax.broadcasted_iota(jnp.int32, moving.shape, 1)
        dz = iw[c + BOX_R + 1] - iw[c + BOX_R - 1]
        dy = jnp.where(row_id == rows - 1, 0.0, pltpu.roll(moving, rows - 1, 0)) - jnp.where(
            row_id == 0, 0.0, pltpu.roll(moving, 1, 0)
        )
        dx = jnp.where(col_id == cols - 1, 0.0, pltpu.roll(moving, cols - 1, 1)) - jnp.where(
            col_id == 0, 0.0, pltpu.roll(moving, 1, 1)
        )
        r_ref[0, c] = factor * dz
        r_ref[1, c] = factor * dy
        r_ref[2, c] = factor * dx
        return 0

    lax.fori_loop(0, BLOCK, plane, 0)


def blur_block(b, weights, r_ref, yx, gy, gx, put):
    rows, cols = r_ref.shape[2], r_ref.shape[3]
    base = b * GROUP

    for k in range(3):

        def strip(s, _):
            row = pl.multiple_of(s * STRIP, STRIP)
            for lane in range(0, cols, 128):
                v = [
                    r_ref[k, base + BOX_R - GAUSS_R + j, pl.ds(row, STRIP), pl.ds(lane, 128)]
                    for j in range(GROUP + 2 * GAUSS_R)
                ]
                for u in range(GROUP):
                    mid = u + GAUSS_R
                    total = weights[0] * v[mid]
                    for o in range(1, GAUSS_R + 1):
                        total = total + weights[o] * (v[mid - o] + v[mid + o])
                    high, low = split2(total)
                    at = u * rows + row
                    yx[k, pl.ds(at, STRIP), pl.ds(lane, 128)] = high
                    yx[k, pl.ds(at, STRIP), pl.ds(cols + lane, 128)] = low
                    yx[k, pl.ds(at, STRIP), pl.ds(2 * cols + lane, 128)] = high
            return 0

        lax.fori_loop(0, rows // STRIP, strip, 0)
    for k in range(3):
        xs = jnp.dot(yx[k], gx[...], preferred_element_type=F32)
        high, low = split2(xs)
        both = jnp.concatenate([high, low, high], axis=0)
        put(k, base, jnp.dot(gy[...], both, preferred_element_type=F32))


def kernel(
    shape, weights, x, by, bx, gy, gx, out, template, loss_out,
    iw, jw, part, got, r_ref, xy, t_ref, yx, out_v, loss, loss_all,
    load_sem, ar_send, ar_recv, halo_send, halo_recv, loss_send, loss_recv, put_sem,
):
    members, size = shape
    planes, rows, cols = x.shape[1:]
    bits = members.bit_length() - 1
    chunks = planes // BLOCK
    stages = 2 * bits - 1
    me = lax.axis_index("subj")
    gz = lax.axis_index("gz")
    z_first, depth = gz * planes, planes * size
    has_low, has_high = gz > 0, gz < size - 1

    def flip(bit):
        mine = (me // (1 << bit)) % 2
        return mine, me + (1 - 2 * mine) * (1 << bit)

    barrier = pltpu.get_barrier_semaphore()
    for bit in range(bits):
        pl.semaphore_signal(barrier, inc=1, device_id={"subj": flip(bit)[1]}, device_id_type=MESH)
    for d in range(1, size):
        peer = lax.rem(gz + d, size)
        pl.semaphore_signal(barrier, inc=1, device_id={"gz": peer}, device_id_type=MESH)

    loads = [
        pltpu.make_async_copy(
            x.at[0, pl.ds(c * BLOCK, BLOCK)], iw.at[pl.ds((c + 1) * BLOCK, BLOCK)], load_sem.at[c]
        )
        for c in range(chunks)
    ]
    for load in loads:
        load.start()
    pl.semaphore_wait(barrier, bits + size - 1)

    half = rows // 2
    plans = []
    for h in range(2):
        order = list(range(bits)) if h == 0 else list(range(bits))[::-1]
        at, length, levels = h * half, half, []
        for bit in order[:-1]:
            mine, peer = flip(bit)
            length //= 2
            kept = at + mine * length
            levels.append((peer, kept, at + (1 - mine) * length, length))
            at = kept
        levels.append((flip(order[-1])[1], at, at, length))
        plans.append(levels)

    def ds(at, length):
        return pl.ds(pl.multiple_of(at, length), length)

    def step(s, h, c):
        deep = s if s < bits else stages - 1 - s
        peer, kept, sent, length = plans[h][deep]
        wide = pl.ds((c + 1) * BLOCK, BLOCK)
        if s >= bits:
            src = jw.at[wide, ds(kept, length)]
            dst = src
        else:
            if s == 0:
                src = x.at[0, pl.ds(c * BLOCK, BLOCK), ds(sent, length)]
            else:
                above = plans[h][s - 1][1]
                src = part.at[s - 1, h, pl.ds(c * BLOCK, BLOCK), ds(sent - above, length)]
            dst = got.at[s, h, pl.ds(c * BLOCK, BLOCK), pl.ds(0, length)]
        return pltpu.make_async_remote_copy(
            src_ref=src,
            dst_ref=dst,
            send_sem=ar_send.at[s, h, c],
            recv_sem=ar_recv.at[s, h, c],
            device_id={"subj": peer},
            device_id_type=MESH,
        )

    def finish(s, c):
        if s == 0:
            loads[c].wait()
        for h in range(2):
            step(s, h, c).wait_recv()
            if s < bits:
                peer, kept, sent, length = plans[h][s]
                here = pl.ds(c * BLOCK, BLOCK)
                new = got[s, h, here, pl.ds(0, length), :]
                if s == 0:
                    old = iw[pl.ds((c + 1) * BLOCK, BLOCK), ds(kept, length), :]
                else:
                    above = plans[h][s - 1][1]
                    old = part[s - 1, h, here, ds(kept - above, length), :]
                if s < bits - 1:
                    part[s, h, here, pl.ds(0, length), :] = old + new
                else:
                    jw[pl.ds((c + 1) * BLOCK, BLOCK), ds(kept, length), :] = (old + new) / members
            if s + 1 < stages:
                step(s + 1, h, c).start()
        if s == stages - 1:
            if c == 0:
                halo(1, 0, 0, "start")
            if c == chunks - 1:
                halo(1, 1, 0, "start")
            pltpu.make_async_copy(
                jw.at[pl.ds((c + 1) * BLOCK, BLOCK)],
                template.at[pl.ds(c * BLOCK, BLOCK)],
                put_sem.at[planes // GROUP + c],
            ).start()

    def halo(which, way, recv, what):
        core = 0 if way == 0 else planes - BLOCK
        there = planes + BLOCK if way == 0 else 0
        wide = iw if which == 0 else jw
        if which == 0:
            src = x.at[0, pl.ds(core, BLOCK)]
        else:
            src = jw.at[pl.ds(core + BLOCK, BLOCK)]
        peer = gz - 1 if way == 0 else gz + 1
        can_send = has_low if way == 0 else has_high
        can_take = has_high if way == 0 else has_low
        copy = pltpu.make_async_remote_copy(
            src_ref=src,
            dst_ref=wide.at[pl.ds(there, BLOCK)],
            send_sem=halo_send.at[which, way],
            recv_sem=halo_recv.at[which, way],
            device_id={"gz": lax.rem(peer + size, size)},
            device_id_type=MESH,
        )

        @pl.when(can_take if recv else can_send)
        def _():
            if what == "start":
                copy.start()
            elif recv:
                copy.wait_recv()
            else:
                copy.wait_send()

    for c in range(chunks):
        for h in range(2):
            step(0, h, c).start()
    halo(0, 0, 0, "start")
    halo(0, 1, 0, "start")

    nothing = jnp.zeros((BLOCK, rows, cols), F32)

    @pl.when(jnp.logical_not(has_low))
    def _():
        iw[pl.ds(0, BLOCK)] = nothing
        jw[pl.ds(0, BLOCK)] = nothing

    @pl.when(jnp.logical_not(has_high))
    def _():
        iw[pl.ds(planes + BLOCK, BLOCK)] = nothing
        jw[pl.ds(planes + BLOCK, BLOCK)] = nothing

    loss[...] = jnp.zeros_like(loss)
    blocks = chunks + 1
    work = [(s, c) for s in range(stages - 1) for c in range(chunks)]

    def pick(i):
        return jnp.where(i < chunks - 1, i + 1, (i - chunks + 1) * chunks)

    def moving_part(i, _):
        for slot in range(blocks):
            todo = [w for j, w in enumerate(work) if j * (blocks + 1) // len(work) == slot]

            @pl.when(i == slot)
            def _(todo=todo, slot=slot):
                for s, c in todo:
                    finish(s, c)
                if slot == chunks - 1:
                    halo(0, 1, 1, "wait")
                if slot == chunks:
                    halo(0, 0, 1, "wait")

        box_block(pick(i), 0, 2, iw, jw, xy, t_ref, by, bx)
        return 0

    lax.fori_loop(0, blocks, moving_part, 0)
    for j, (s, c) in enumerate(work):
        if j * (blocks + 1) // len(work) == blocks:
            finish(s, c)

    def target_part(i, _):
        for slot in range(blocks):

            @pl.when(i == slot)
            def _(slot=slot):
                if slot == 0:
                    finish(stages - 1, 0)
                if slot + 1 < chunks:
                    finish(stages - 1, slot + 1)
                if slot == chunks - 1:
                    halo(1, 1, 1, "wait")
                if slot == chunks:
                    halo(1, 0, 1, "wait")

        b = pick(i)
        box_block(b, 2, 3, iw, jw, xy, t_ref, by, bx)
        force_block(b, z_first, depth, planes, iw, jw, r_ref, t_ref, loss)
        return 0

    lax.fori_loop(0, blocks, target_part, 0)

    total = jnp.zeros((8, 128), F32)
    for row in range(0, rows, 8):
        for lane in range(0, cols, 128):
            total = total + loss[pl.ds(row, 8), pl.ds(lane, 128)]
    loss_all[gz] = total

    def share(d):
        return pltpu.make_async_remote_copy(
            src_ref=loss_all.at[gz],
            dst_ref=loss_all.at[gz],
            send_sem=loss_send.at[d],
            recv_sem=loss_recv.at[d],
            device_id={"gz": lax.rem(gz + d, size)},
            device_id_type=MESH,
        )

    for d in range(1, size):
        share(d).start()

    def put(k, base, value):
        out_v[k, pl.ds(base, GROUP)] = jnp.reshape(value, (GROUP, rows, cols))

    def put_copy(g):
        at = pl.ds(g * GROUP, GROUP)
        return pltpu.make_async_copy(out_v.at[:, at], out.at[0, :, at], put_sem.at[g])

    def blur(g, _):
        blur_block(g, weights, r_ref, yx, gy, gx, put)
        put_copy(g).start()
        return 0

    lax.fori_loop(0, planes // GROUP, blur, 0)

    for d in range(1, size):
        share(d).wait_recv()
    sims = loss_all[0]
    for k in range(1, size):
        sims = sims + loss_all[k]
    loss_out[0] = -jnp.sum(sims) / float(depth * rows * cols)

    for g in range(planes // GROUP):
        put_copy(g).wait()
    for c in range(chunks):
        pltpu.make_async_copy(
            jw.at[pl.ds((c + 1) * BLOCK, BLOCK)],
            template.at[pl.ds(c * BLOCK, BLOCK)],
            put_sem.at[planes // GROUP + c],
        ).wait()
    for d in range(1, size):
        share(d).wait_send()
    for s in range(stages):
        for h in range(2):
            for c in range(chunks):
                step(s, h, c).wait_send()
    for which in range(2):
        for way in range(2):
            halo(which, way, 0, "wait")


def on_device(warped):
    planes, rows, cols = warped.shape[1:]
    members, size = lax.axis_size("subj"), lax.axis_size("gz")
    bits = members.bit_length() - 1
    assert members == 1 << bits and bits > 1 and planes % BLOCK == 0
    by, bx, gy, gx, weights = bands(rows, cols)
    chunks = planes // BLOCK
    stages = 2 * bits - 1
    grows = GROUP * rows
    vmem = pl.BlockSpec(memory_space=pltpu.VMEM)
    anywhere = pl.BlockSpec(memory_space=pl.ANY)
    cells = planes * rows * cols
    dma = pltpu.SemaphoreType.DMA
    force, template, loss = pl.pallas_call(
        functools.partial(kernel, (members, size), weights),
        out_shape=(
            jax.ShapeDtypeStruct((1, 3, planes, rows, cols), F32),
            jax.ShapeDtypeStruct((planes, rows, cols), F32),
            jax.ShapeDtypeStruct((1,), F32),
        ),
        in_specs=[anywhere] + [vmem] * 4,
        out_specs=(anywhere, anywhere, pl.BlockSpec(memory_space=pltpu.SMEM)),
        scratch_shapes=[
            pltpu.VMEM((planes + 2 * BLOCK, rows, cols), F32),
            pltpu.VMEM((planes + 2 * BLOCK, rows, cols), F32),
            pltpu.VMEM((bits - 1, 2, planes, rows // 4, cols), F32),
            pltpu.VMEM((bits, 2, planes, rows // 4, cols), F32),
            pltpu.VMEM((3, planes + BLOCK, rows, cols), F32),
            pltpu.VMEM((3, BLOCK // GROUP, 3 * grows, cols), BF16),
            pltpu.VMEM((5, (planes + BLOCK) * rows, cols), F32),
            pltpu.VMEM((3, grows, 3 * cols), BF16),
            pltpu.VMEM((3, planes, rows, cols), F32),
            pltpu.VMEM((rows, cols), F32),
            pltpu.VMEM((size, 8, 128), F32),
            dma((chunks,)),
            dma((stages, 2, chunks)),
            dma((stages, 2, chunks)),
            dma((2, 2)),
            dma((2, 2)),
            dma((size,)),
            dma((size,)),
            dma((planes // GROUP + chunks,)),
        ],
        compiler_params=pltpu.CompilerParams(
            collective_id=0, has_side_effects=True, vmem_limit_bytes=60 * 1024 * 1024
        ),
        cost_estimate=pl.CostEstimate(
            flops=300 * cells, bytes_accessed=20 * cells, transcendentals=0
        ),
    )(warped, by, bx, gy, gx)
    return (force, template, loss)


def solution(mesh):
    placed = (P("subj", "gz", None, None),)
    return jax.shard_map(
        on_device,
        mesh=mesh,
        in_specs=placed,
        out_specs=(P("subj", None, "gz", None, None), P("gz", None, None), P("subj")),
        check_vma=False,
    )
```

```python
import functools
import math

import jax
import jax.numpy as jnp
import ml_dtypes
import numpy as np
from jax import lax
from jax.experimental import pallas as pl
from jax.experimental.pallas import tpu as pltpu
from jax.sharding import PartitionSpec as P

BOX_R = 4
GAUSS_R = 3
EPS = 1e-05
BLOCK = 8
GROUP = 4
STRIP = 16
PIECE = 4
F32 = jnp.float32
BF16 = jnp.bfloat16
MESH = pl.DeviceIdType.MESH


def bands(rows, cols):
    bumps = np.array([math.exp(-(k * k) / 8.0) for k in range(-GAUSS_R, GAUSS_R + 1)])
    bumps = bumps / bumps.sum()

    def band(n, weights, radius):
        out = np.zeros((n, n), np.float32)
        for k in range(-radius, radius + 1):
            out += np.diag(np.full(n - abs(k), weights[k + radius], np.float32), k)
        return out

    def high_low(m):
        high = m.astype(ml_dtypes.bfloat16)
        low = (m - high.astype(np.float32)).astype(ml_dtypes.bfloat16)
        return high, low

    ones = np.ones(2 * BOX_R + 1)
    eye = np.eye(GROUP, dtype=np.float32)
    box_y = np.kron(eye, band(rows, ones, BOX_R)).astype(ml_dtypes.bfloat16)
    box_x = band(cols, ones, BOX_R).astype(ml_dtypes.bfloat16)
    gy_high, gy_low = high_low(np.kron(eye, band(rows, bumps, GAUSS_R)))
    gx_high, gx_low = high_low(band(cols, bumps, GAUSS_R))
    return (
        np.concatenate([box_y] * 3, axis=1),
        np.concatenate([box_x] * 3, axis=0),
        np.concatenate([gy_high, gy_high, gy_low], axis=1),
        np.concatenate([gx_high, gx_high, gx_low], axis=0),
        [float(b) for b in bumps[GAUSS_R:]],
    )


def split3(v):
    a = v.astype(BF16)
    r = v - a.astype(F32)
    b = r.astype(BF16)
    c = (r - b.astype(F32)).astype(BF16)
    return a, b, c


def split2(v):
    a = v.astype(BF16)
    return a, (v - a.astype(F32)).astype(BF16)


def windows(planes):
    n = BLOCK
    span = 2 * BOX_R + 1
    head = [None] * (n + 1)
    acc = planes[n - 1]
    head[n - 1] = acc
    for i in range(n - 2, -1, -1):
        acc = acc + planes[i]
        head[i] = acc
    out = []
    tail = None
    for i in range(n):
        tail = planes[n + i] if tail is None else tail + planes[n + i]
        out.append(head[i] + tail)
    assert span == n + 1
    return out


def box_block(b, first, count, iw, jw, xy, t_ref, by, bx):
    rows, cols = iw.shape[1], iw.shape[2]
    base = b * BLOCK
    grows = GROUP * rows
    span = BLOCK + 2 * BOX_R

    def strip(s, _):
        row = pl.multiple_of(s * STRIP, STRIP)
        for lane in range(0, cols, 128):
            iv = [iw[base + k, pl.ds(row, STRIP), pl.ds(lane, 128)] for k in range(span)]
            if first + count > 2:
                jv = [jw[base + k, pl.ds(row, STRIP), pl.ds(lane, 128)] for k in range(span)]
            for v in range(first, first + count):
                if v == 0:
                    vol = iv
                elif v == 1:
                    vol = [a * a for a in iv]
                elif v == 2:
                    vol = jv
                elif v == 3:
                    vol = [a * a for a in jv]
                else:
                    vol = [a * c for a, c in zip(iv, jv)]
                for w, total in enumerate(windows(vol)):
                    g, u = w // GROUP, w % GROUP
                    for k, piece in enumerate(split3(total)):
                        at = k * grows + u * rows
                        xy[v - first, g, pl.ds(at + row, STRIP), pl.ds(lane, 128)] = piece
        return 0

    lax.fori_loop(0, rows // STRIP, strip, 0)

    def group(g, _):
        at = pl.multiple_of(b * BLOCK * rows + g * grows, grows)
        for v in range(count):
            ys = jnp.dot(by[...], xy[v, g], preferred_element_type=F32)
            xs = jnp.concatenate(split3(ys), axis=1)
            t_ref[first + v, pl.ds(at, grows), :] = jnp.dot(
                xs, bx[...], preferred_element_type=F32
            )
        return 0

    lax.fori_loop(0, BLOCK // GROUP, group, 0)


def force_block(b, z_first, depth, planes, iw, jw, r_ref, t_ref, loss):
    rows, cols = iw.shape[1], iw.shape[2]
    scale = 1.0 / float((2 * BOX_R + 1) ** 3)

    def plane(u, _):
        c = b * BLOCK + u
        at = pl.multiple_of(c * rows, rows)
        m = [t_ref[v, pl.ds(at, rows), :] * scale for v in range(5)]
        mi, mj = m[0], m[2]
        var_i = m[1] - mi * mi
        var_j = m[3] - mj * mj
        cc = m[4] - mi * mj
        moving = iw[c + BOX_R]
        target = jw[c + BOX_R]
        q = cc / (var_i * var_j + EPS)
        core = c - BOX_R
        z = z_first + core
        owned = jnp.logical_and(core >= 0, core < planes)
        loss[...] += jnp.where(owned, cc * q, 0.0)
        factor = q * ((target - mj) - cc / (var_i + EPS) * (moving - mi))
        inside = jnp.logical_and(z >= 0, z < depth)
        factor = jnp.where(inside, factor, 0.0)
        row_id = lax.broadcasted_iota(jnp.int32, moving.shape, 0)
        col_id = lax.broadcasted_iota(jnp.int32, moving.shape, 1)
        dz = iw[c + BOX_R + 1] - iw[c + BOX_R - 1]
        dy = jnp.where(row_id == rows - 1, 0.0, pltpu.roll(moving, rows - 1, 0)) - jnp.where(
            row_id == 0, 0.0, pltpu.roll(moving, 1, 0)
        )
        dx = jnp.where(col_id == cols - 1, 0.0, pltpu.roll(moving, cols - 1, 1)) - jnp.where(
            col_id == 0, 0.0, pltpu.roll(moving, 1, 1)
        )
        r_ref[0, c] = factor * dz
        r_ref[1, c] = factor * dy
        r_ref[2, c] = factor * dx
        return 0

    lax.fori_loop(0, BLOCK, plane, 0)


def blur_block(b, weights, r_ref, yx, gy, gx, put):
    rows, cols = r_ref.shape[2], r_ref.shape[3]
    base = b * GROUP

    for k in range(3):

        def strip(s, _):
            row = pl.multiple_of(s * STRIP, STRIP)
            for lane in range(0, cols, 128):
                v = [
                    r_ref[k, base + BOX_R - GAUSS_R + j, pl.ds(row, STRIP), pl.ds(lane, 128)]
                    for j in range(GROUP + 2 * GAUSS_R)
                ]
                for u in range(GROUP):
                    mid = u + GAUSS_R
                    total = weights[0] * v[mid]
                    for o in range(1, GAUSS_R + 1):
                        total = total + weights[o] * (v[mid - o] + v[mid + o])
                    high, low = split2(total)
                    at = u * rows + row
                    yx[k, pl.ds(at, STRIP), pl.ds(lane, 128)] = high
                    yx[k, pl.ds(at, STRIP), pl.ds(cols + lane, 128)] = low
                    yx[k, pl.ds(at, STRIP), pl.ds(2 * cols + lane, 128)] = high
            return 0

        lax.fori_loop(0, rows // STRIP, strip, 0)
    for k in range(3):
        xs = jnp.dot(yx[k], gx[...], preferred_element_type=F32)
        high, low = split2(xs)
        both = jnp.concatenate([high, low, high], axis=0)
        put(k, base, jnp.dot(gy[...], both, preferred_element_type=F32))


def kernel(
    shape, x, by, bx, raw, template, loss_out,
    iw, jw, part, got, r_ref, xy, t_ref, loss, loss_all,
    load_sem, ar_send, ar_recv, halo_send, halo_recv, loss_send, loss_recv, put_sem,
):
    members, size = shape
    planes, rows, cols = x.shape[1:]
    bits = members.bit_length() - 1
    chunks = planes // BLOCK
    pieces = planes // PIECE
    stages = 2 * bits - 1
    me = lax.axis_index("subj")
    gz = lax.axis_index("gz")
    z_first, depth = gz * planes, planes * size
    has_low, has_high = gz > 0, gz < size - 1

    def flip(bit):
        mine = (me // (1 << bit)) % 2
        return mine, me + (1 - 2 * mine) * (1 << bit)

    barrier = pltpu.get_barrier_semaphore()
    for bit in range(bits):
        pl.semaphore_signal(barrier, inc=1, device_id={"subj": flip(bit)[1]}, device_id_type=MESH)
    for d in range(1, size):
        peer = lax.rem(gz + d, size)
        pl.semaphore_signal(barrier, inc=1, device_id={"gz": peer}, device_id_type=MESH)

    loads = [
        pltpu.make_async_copy(
            x.at[0, pl.ds(c * BLOCK, BLOCK)], iw.at[pl.ds((c + 1) * BLOCK, BLOCK)], load_sem.at[c]
        )
        for c in range(chunks)
    ]
    for load in loads:
        load.start()
    pl.semaphore_wait(barrier, bits + size - 1)

    half = rows // 2
    plans = []
    for h in range(2):
        order = list(range(bits)) if h == 0 else list(range(bits))[::-1]
        at, length, levels = h * half, half, []
        for bit in order[:-1]:
            mine, peer = flip(bit)
            length //= 2
            kept = at + mine * length
            levels.append((peer, kept, at + (1 - mine) * length, length))
            at = kept
        levels.append((flip(order[-1])[1], at, at, length))
        plans.append(levels)

    def ds(at, length):
        return pl.ds(pl.multiple_of(at, length), length)

    def step(s, h, c):
        deep = s if s < bits else stages - 1 - s
        peer, kept, sent, length = plans[h][deep]
        wide = pl.ds(BLOCK + c * PIECE, PIECE)
        if s >= bits:
            src = jw.at[wide, ds(kept, length)]
            dst = src
        else:
            if s == 0:
                src = x.at[0, pl.ds(c * PIECE, PIECE), ds(sent, length)]
            else:
                above = plans[h][s - 1][1]
                src = part.at[s - 1, h, pl.ds(c * PIECE, PIECE), ds(sent - above, length)]
            dst = got.at[s, h, pl.ds(c * PIECE, PIECE), pl.ds(0, length)]
        return pltpu.make_async_remote_copy(
            src_ref=src,
            dst_ref=dst,
            send_sem=ar_send.at[s, h, c],
            recv_sem=ar_recv.at[s, h, c],
            device_id={"subj": peer},
            device_id_type=MESH,
        )

    def finish(s, c):
        for h in range(2):
            step(s, h, c).wait_recv()
            if s < bits:
                peer, kept, sent, length = plans[h][s]
                here = pl.ds(c * PIECE, PIECE)
                core = pl.ds(BLOCK + c * PIECE, PIECE)
                new = got[s, h, here, pl.ds(0, length), :]
                if s == 0:
                    old = iw[core, ds(kept, length), :]
                else:
                    above = plans[h][s - 1][1]
                    old = part[s - 1, h, here, ds(kept - above, length), :]
                if s < bits - 1:
                    part[s, h, here, pl.ds(0, length), :] = old + new
                else:
                    jw[core, ds(kept, length), :] = (old + new) / members
            if s + 1 < stages:
                step(s + 1, h, c).start()

    def halo(which, way, recv, what):
        core = 0 if way == 0 else planes - BLOCK
        there = planes + BLOCK if way == 0 else 0
        wide = iw if which == 0 else jw
        if which == 0:
            src = x.at[0, pl.ds(core, BLOCK)]
        else:
            src = jw.at[pl.ds(core + BLOCK, BLOCK)]
        peer = gz - 1 if way == 0 else gz + 1
        can_send = has_low if way == 0 else has_high
        can_take = has_high if way == 0 else has_low
        copy = pltpu.make_async_remote_copy(
            src_ref=src,
            dst_ref=wide.at[pl.ds(there, BLOCK)],
            send_sem=halo_send.at[which, way],
            recv_sem=halo_recv.at[which, way],
            device_id={"gz": lax.rem(peer + size, size)},
            device_id_type=MESH,
        )

        @pl.when(can_take if recv else can_send)
        def _():
            if what == "start":
                copy.start()
            elif recv:
                copy.wait_recv()
            else:
                copy.wait_send()

    edge = BLOCK // PIECE
    order = list(range(edge)) + list(range(pieces - edge, pieces))
    order += list(range(edge, pieces - edge))
    ahead = 4

    def first(pos):
        if pos < pieces:
            for h in range(2):
                step(0, h, order[pos]).start()

    for pos in range(ahead):
        first(pos)
    halo(0, 0, 0, "start")
    halo(0, 1, 0, "start")

    nothing = jnp.zeros((BLOCK, rows, cols), F32)

    @pl.when(jnp.logical_not(has_low))
    def _():
        iw[pl.ds(0, BLOCK)] = nothing
        jw[pl.ds(0, BLOCK)] = nothing

    @pl.when(jnp.logical_not(has_high))
    def _():
        iw[pl.ds(planes + BLOCK, BLOCK)] = nothing
        jw[pl.ds(planes + BLOCK, BLOCK)] = nothing

    loss[...] = jnp.zeros_like(loss)
    blocks = chunks + 1
    last = 2 * (stages - 1)
    events = sorted((pos + 2 * s, -s, pos) for s in range(stages) for pos in range(pieces))

    def need(slot):
        b = 0 if slot == 0 else chunks if slot == 1 else slot - 1
        cells = [c for c in range((b - 1) * edge, (b + 1) * edge) if 0 <= c < pieces]
        return last + max(order.index(c) for c in cells)

    def place(key):
        if key < last + 2:
            return 0, key * blocks // (last + 2)
        if key <= last + 2 * edge - 1:
            return 1, 0
        if key == last + 2 * edge:
            return 2, 0
        if key == last + 2 * edge + 1:
            return 1, 1
        return 1, min(t for t in range(blocks) if need(t) >= key)

    def serve(kind, slot):
        for key, s, pos in events:
            if place(key) == (kind, slot):
                finish(-s, order[pos])
                if s == 0:
                    first(pos + ahead)
                if -s == stages - 1 and pos == edge - 1:
                    halo(1, 0, 0, "start")
                if -s == stages - 1 and pos == 2 * edge - 1:
                    halo(1, 1, 0, "start")

    for load in loads:
        load.wait()

    def moving_part(i, _):
        for slot in range(blocks):

            @pl.when(i == slot)
            def _(slot=slot):
                serve(0, slot)
                if slot == chunks - 1:
                    halo(0, 1, 1, "wait")
                if slot == chunks:
                    halo(0, 0, 1, "wait")

        b = jnp.where(i < chunks - 1, i + 1, (i - chunks + 1) * chunks)
        box_block(b, 0, 2, iw, jw, xy, t_ref, by, bx)
        return 0

    lax.fori_loop(0, blocks, moving_part, 0)

    def raw_copy(b):
        at = pl.ds(b * BLOCK, BLOCK)
        return pltpu.make_async_copy(r_ref.at[:, at], raw.at[:, at], put_sem.at[b])

    def target_part(i, _):
        for slot in range(blocks):

            @pl.when(i == slot)
            def _(slot=slot):
                serve(1, slot)
                if slot == 0:
                    halo(1, 1, 1, "wait")
                if slot == 1:
                    halo(1, 0, 1, "wait")

        b = jnp.where(i == 0, 0, jnp.where(i == 1, chunks, i - 1))
        box_block(b, 2, 3, iw, jw, xy, t_ref, by, bx)

        @pl.when(i == 0)
        def _():
            serve(2, 0)

        force_block(b, z_first, depth, planes, iw, jw, r_ref, t_ref, loss)
        raw_copy(b).start()
        return 0

    lax.fori_loop(0, blocks, target_part, 0)
    whole = pltpu.make_async_copy(jw.at[pl.ds(BLOCK, planes)], template, put_sem.at[blocks])
    whole.start()

    total = jnp.zeros((8, 128), F32)
    for row in range(0, rows, 8):
        for lane in range(0, cols, 128):
            total = total + loss[pl.ds(row, 8), pl.ds(lane, 128)]
    loss_all[gz] = total

    def share(d):
        return pltpu.make_async_remote_copy(
            src_ref=loss_all.at[gz],
            dst_ref=loss_all.at[gz],
            send_sem=loss_send.at[d],
            recv_sem=loss_recv.at[d],
            device_id={"gz": lax.rem(gz + d, size)},
            device_id_type=MESH,
        )

    for d in range(1, size):
        share(d).start()

    for d in range(1, size):
        share(d).wait_recv()
    sims = loss_all[0]
    for k in range(1, size):
        sims = sims + loss_all[k]
    loss_out[0] = -jnp.sum(sims) / float(depth * rows * cols)

    for b in range(blocks):
        raw_copy(b).wait()
    whole.wait()
    for d in range(1, size):
        share(d).wait_send()
    for s in range(stages):
        for h in range(2):
            for c in range(pieces):
                step(s, h, c).wait_send()
    for which in range(2):
        for way in range(2):
            halo(which, way, 0, "wait")


def blur_kernel(weights, raw, mean, gy, gx, out, template, r_ref, yx, out_v, load_sem, put_sem):
    planes, rows, cols = out.shape[2:]
    blocks = raw.shape[1] // BLOCK

    def load(b):
        at = pl.ds(b * BLOCK, BLOCK)
        return pltpu.make_async_copy(raw.at[:, at], r_ref.at[:, at], load_sem.at[b])

    for b in range(blocks):
        load(b).start()
    whole = pltpu.make_async_copy(mean, template, load_sem.at[blocks])
    whole.start()
    load(0).wait()

    def put(k, base, value):
        out_v[k, pl.ds(base, GROUP)] = jnp.reshape(value, (GROUP, rows, cols))

    def put_copy(g):
        at = pl.ds(g * GROUP, GROUP)
        return pltpu.make_async_copy(out_v.at[:, at], out.at[0, :, at], put_sem.at[g])

    def blur(g, _):
        @pl.when(lax.rem(g, BLOCK // GROUP) == 0)
        def _():
            load(g // (BLOCK // GROUP) + 1).wait()

        blur_block(g, weights, r_ref, yx, gy, gx, put)
        put_copy(g).start()
        return 0

    lax.fori_loop(0, planes // GROUP, blur, 0)
    for g in range(planes // GROUP):
        put_copy(g).wait()
    whole.wait()


def on_device(warped):
    planes, rows, cols = warped.shape[1:]
    members, size = lax.axis_size("subj"), lax.axis_size("gz")
    bits = members.bit_length() - 1
    assert members == 1 << bits and bits > 1 and planes % BLOCK == 0
    by, bx, gy, gx, weights = bands(rows, cols)
    chunks, pieces = planes // BLOCK, planes // PIECE
    stages = 2 * bits - 1
    grows = GROUP * rows
    vmem = pl.BlockSpec(memory_space=pltpu.VMEM)
    anywhere = pl.BlockSpec(memory_space=pl.ANY)
    cells = planes * rows * cols
    dma = pltpu.SemaphoreType.DMA
    raw_shape = (3, planes + BLOCK, rows, cols)
    raw, mean, loss = pl.pallas_call(
        functools.partial(kernel, (members, size)),
        out_shape=(
            jax.ShapeDtypeStruct(raw_shape, F32),
            jax.ShapeDtypeStruct((planes, rows, cols), F32),
            jax.ShapeDtypeStruct((1,), F32),
        ),
        in_specs=[anywhere] + [vmem] * 2,
        out_specs=(anywhere, anywhere, pl.BlockSpec(memory_space=pltpu.SMEM)),
        scratch_shapes=[
            pltpu.VMEM((planes + 2 * BLOCK, rows, cols), F32),
            pltpu.VMEM((planes + 2 * BLOCK, rows, cols), F32),
            pltpu.VMEM((bits - 1, 2, planes, rows // 4, cols), F32),
            pltpu.VMEM((bits, 2, planes, rows // 4, cols), F32),
            pltpu.VMEM(raw_shape, F32),
            pltpu.VMEM((3, BLOCK // GROUP, 3 * grows, cols), BF16),
            pltpu.VMEM((5, (planes + BLOCK) * rows, cols), F32),
            pltpu.VMEM((rows, cols), F32),
            pltpu.VMEM((size, 8, 128), F32),
            dma((chunks,)),
            dma((stages, 2, pieces)),
            dma((stages, 2, pieces)),
            dma((2, 2)),
            dma((2, 2)),
            dma((size,)),
            dma((size,)),
            dma((chunks + 2,)),
        ],
        compiler_params=pltpu.CompilerParams(
            collective_id=0, has_side_effects=True, vmem_limit_bytes=60 * 1024 * 1024
        ),
        cost_estimate=pl.CostEstimate(
            flops=200 * cells, bytes_accessed=20 * cells, transcendentals=0
        ),
    )(warped, by, bx)
    force, template = pl.pallas_call(
        functools.partial(blur_kernel, weights),
        out_shape=(
            jax.ShapeDtypeStruct((1, 3, planes, rows, cols), F32),
            jax.ShapeDtypeStruct((planes, rows, cols), F32),
        ),
        in_specs=[anywhere, anywhere, vmem, vmem],
        out_specs=(anywhere, anywhere),
        scratch_shapes=[
            pltpu.VMEM(raw_shape, F32),
            pltpu.VMEM((3, grows, 3 * cols), BF16),
            pltpu.VMEM((3, planes, rows, cols), F32),
            dma((chunks + 2,)),
            dma((planes // GROUP,)),
        ],
        compiler_params=pltpu.CompilerParams(vmem_limit_bytes=60 * 1024 * 1024),
        cost_estimate=pl.CostEstimate(
            flops=100 * cells, bytes_accessed=32 * cells, transcendentals=0
        ),
    )(raw, mean, gy, gx)
    return (force, template, loss)


def solution(mesh):
    placed = (P("subj", "gz", None, None),)
    return jax.shard_map(
        on_device,
        mesh=mesh,
        in_specs=placed,
        out_specs=(P("subj", None, "gz", None, None), P("gz", None, None), P("subj")),
        check_vma=False,
    )
```

```python
import functools
import math

import jax
import jax.numpy as jnp
import ml_dtypes
import numpy as np
from jax import lax
from jax.experimental import pallas as pl
from jax.experimental.pallas import tpu as pltpu
from jax.sharding import PartitionSpec as P

BOX_R = 4
GAUSS_R = 3
EPS = 1e-05
BLOCK = 8
GROUP = 4
STRIP = 16
PIECE = 4
F32 = jnp.float32
BF16 = jnp.bfloat16
MESH = pl.DeviceIdType.MESH


def bands(rows, cols):
    bumps = np.array([math.exp(-(k * k) / 8.0) for k in range(-GAUSS_R, GAUSS_R + 1)])
    bumps = bumps / bumps.sum()

    def band(n, weights, radius):
        out = np.zeros((n, n), np.float32)
        for k in range(-radius, radius + 1):
            out += np.diag(np.full(n - abs(k), weights[k + radius], np.float32), k)
        return out

    def high_low(m):
        high = m.astype(ml_dtypes.bfloat16)
        low = (m - high.astype(np.float32)).astype(ml_dtypes.bfloat16)
        return high, low

    ones = np.ones(2 * BOX_R + 1)
    eye = np.eye(GROUP, dtype=np.float32)
    box_y = np.kron(eye, band(rows, ones, BOX_R)).astype(ml_dtypes.bfloat16)
    box_x = band(cols, ones, BOX_R).astype(ml_dtypes.bfloat16)
    gy_high, gy_low = high_low(np.kron(eye, band(rows, bumps, GAUSS_R)))
    gx_high, gx_low = high_low(band(cols, bumps, GAUSS_R))
    return (
        np.concatenate([box_y] * 3, axis=1),
        np.concatenate([box_x] * 3, axis=0),
        np.concatenate([gy_high, gy_high, gy_low], axis=1),
        np.concatenate([gx_high, gx_high, gx_low], axis=0),
        [float(b) for b in bumps[GAUSS_R:]],
    )


def split3(v):
    a = v.astype(BF16)
    r = v - a.astype(F32)
    b = r.astype(BF16)
    c = (r - b.astype(F32)).astype(BF16)
    return a, b, c


def split2(v):
    a = v.astype(BF16)
    return a, (v - a.astype(F32)).astype(BF16)


def windows(planes):
    n = BLOCK
    span = 2 * BOX_R + 1
    head = [None] * (n + 1)
    acc = planes[n - 1]
    head[n - 1] = acc
    for i in range(n - 2, -1, -1):
        acc = acc + planes[i]
        head[i] = acc
    out = []
    tail = None
    for i in range(n):
        tail = planes[n + i] if tail is None else tail + planes[n + i]
        out.append(head[i] + tail)
    assert span == n + 1
    return out


def box_block(b, first, count, iw, jw, xy, t_ref, by, bx):
    rows, cols = iw.shape[1], iw.shape[2]
    base = b * BLOCK
    grows = GROUP * rows
    span = BLOCK + 2 * BOX_R

    def strip(s, _):
        row = pl.multiple_of(s * STRIP, STRIP)
        for lane in range(0, cols, 128):
            iv = [iw[base + k, pl.ds(row, STRIP), pl.ds(lane, 128)] for k in range(span)]
            if first + count > 2:
                jv = [jw[base + k, pl.ds(row, STRIP), pl.ds(lane, 128)] for k in range(span)]
            for v in range(first, first + count):
                if v == 0:
                    vol = iv
                elif v == 1:
                    vol = [a * a for a in iv]
                elif v == 2:
                    vol = jv
                elif v == 3:
                    vol = [a * a for a in jv]
                else:
                    vol = [a * c for a, c in zip(iv, jv)]
                for w, total in enumerate(windows(vol)):
                    g, u = w // GROUP, w % GROUP
                    for k, piece in enumerate(split3(total)):
                        at = k * grows + u * rows
                        xy[v - first, g, pl.ds(at + row, STRIP), pl.ds(lane, 128)] = piece
        return 0

    lax.fori_loop(0, rows // STRIP, strip, 0)

    def group(g, _):
        at = pl.multiple_of(b * BLOCK * rows + g * grows, grows)
        for v in range(count):
            ys = jnp.dot(by[...], xy[v, g], preferred_element_type=F32)
            xs = jnp.concatenate(split3(ys), axis=1)
            t_ref[first + v, pl.ds(at, grows), :] = jnp.dot(
                xs, bx[...], preferred_element_type=F32
            )
        return 0

    lax.fori_loop(0, BLOCK // GROUP, group, 0)


def force_block(b, z_first, depth, planes, iw, jw, r_ref, t_ref, loss):
    rows, cols = iw.shape[1], iw.shape[2]
    scale = 1.0 / float((2 * BOX_R + 1) ** 3)

    def plane(u, _):
        c = b * BLOCK + u
        at = pl.multiple_of(c * rows, rows)
        m = [t_ref[v, pl.ds(at, rows), :] * scale for v in range(5)]
        mi, mj = m[0], m[2]
        var_i = m[1] - mi * mi
        var_j = m[3] - mj * mj
        cc = m[4] - mi * mj
        moving = iw[c + BOX_R]
        target = jw[c + BOX_R]
        q = cc / (var_i * var_j + EPS)
        core = c - BOX_R
        z = z_first + core
        owned = jnp.logical_and(core >= 0, core < planes)
        loss[...] += jnp.where(owned, cc * q, 0.0)
        factor = q * ((target - mj) - cc / (var_i + EPS) * (moving - mi))
        inside = jnp.logical_and(z >= 0, z < depth)
        factor = jnp.where(inside, factor, 0.0)
        row_id = lax.broadcasted_iota(jnp.int32, moving.shape, 0)
        col_id = lax.broadcasted_iota(jnp.int32, moving.shape, 1)
        dz = iw[c + BOX_R + 1] - iw[c + BOX_R - 1]
        dy = jnp.where(row_id == rows - 1, 0.0, pltpu.roll(moving, rows - 1, 0)) - jnp.where(
            row_id == 0, 0.0, pltpu.roll(moving, 1, 0)
        )
        dx = jnp.where(col_id == cols - 1, 0.0, pltpu.roll(moving, cols - 1, 1)) - jnp.where(
            col_id == 0, 0.0, pltpu.roll(moving, 1, 1)
        )
        r_ref[0, c] = factor * dz
        r_ref[1, c] = factor * dy
        r_ref[2, c] = factor * dx
        return 0

    lax.fori_loop(0, BLOCK, plane, 0)


def blur_block(b, weights, r_ref, yx, gy, gx, put):
    rows, cols = r_ref.shape[2], r_ref.shape[3]
    base = b * GROUP

    for k in range(3):

        def strip(s, _):
            row = pl.multiple_of(s * STRIP, STRIP)
            for lane in range(0, cols, 128):
                v = [
                    r_ref[k, base + BOX_R - GAUSS_R + j, pl.ds(row, STRIP), pl.ds(lane, 128)]
                    for j in range(GROUP + 2 * GAUSS_R)
                ]
                for u in range(GROUP):
                    mid = u + GAUSS_R
                    total = weights[0] * v[mid]
                    for o in range(1, GAUSS_R + 1):
                        total = total + weights[o] * (v[mid - o] + v[mid + o])
                    high, low = split2(total)
                    at = u * rows + row
                    yx[k, pl.ds(at, STRIP), pl.ds(lane, 128)] = high
                    yx[k, pl.ds(at, STRIP), pl.ds(cols + lane, 128)] = low
                    yx[k, pl.ds(at, STRIP), pl.ds(2 * cols + lane, 128)] = high
            return 0

        lax.fori_loop(0, rows // STRIP, strip, 0)
    for k in range(3):
        xs = jnp.dot(yx[k], gx[...], preferred_element_type=F32)
        high, low = split2(xs)
        both = jnp.concatenate([high, low, high], axis=0)
        put(k, base, jnp.dot(gy[...], both, preferred_element_type=F32))


def kernel(
    shape, x, by, bx, raw, template, loss_out,
    iw, jw, part, got, r_ref, xy, t_ref, loss, loss_all,
    load_sem, ar_send, ar_recv, halo_send, halo_recv, loss_send, loss_recv, put_sem,
):
    members, size = shape
    planes, rows, cols = x.shape[1:]
    bits = members.bit_length() - 1
    chunks = planes // BLOCK
    pieces = planes // PIECE
    stages = 2 * bits - 1
    me = lax.axis_index("subj")
    gz = lax.axis_index("gz")
    z_first, depth = gz * planes, planes * size
    has_low, has_high = gz > 0, gz < size - 1

    def flip(bit):
        mine = (me // (1 << bit)) % 2
        return mine, me + (1 - 2 * mine) * (1 << bit)

    barrier = pltpu.get_barrier_semaphore()
    for bit in range(bits):
        pl.semaphore_signal(barrier, inc=1, device_id={"subj": flip(bit)[1]}, device_id_type=MESH)
    for d in range(1, size):
        peer = lax.rem(gz + d, size)
        pl.semaphore_signal(barrier, inc=1, device_id={"gz": peer}, device_id_type=MESH)

    loads = [
        pltpu.make_async_copy(
            x.at[0, pl.ds(c * BLOCK, BLOCK)], iw.at[pl.ds((c + 1) * BLOCK, BLOCK)], load_sem.at[c]
        )
        for c in range(chunks)
    ]
    for load in loads:
        load.start()
    pl.semaphore_wait(barrier, bits + size - 1)

    half = rows // 2
    plans = []
    for h in range(2):
        order = list(range(bits)) if h == 0 else list(range(bits))[::-1]
        at, length, levels = h * half, half, []
        for bit in order[:-1]:
            mine, peer = flip(bit)
            length //= 2
            kept = at + mine * length
            levels.append((peer, kept, at + (1 - mine) * length, length))
            at = kept
        levels.append((flip(order[-1])[1], at, at, length))
        plans.append(levels)

    def ds(at, length):
        return pl.ds(pl.multiple_of(at, length), length)

    def step(s, h, c):
        deep = s if s < bits else stages - 1 - s
        peer, kept, sent, length = plans[h][deep]
        wide = pl.ds(BLOCK + c * PIECE, PIECE)
        if s >= bits:
            src = jw.at[wide, ds(kept, length)]
            dst = src
        else:
            if s == 0:
                src = x.at[0, pl.ds(c * PIECE, PIECE), ds(sent, length)]
            else:
                above = plans[h][s - 1][1]
                src = part.at[s - 1, h, pl.ds(c * PIECE, PIECE), ds(sent - above, length)]
            dst = got.at[s, h, pl.ds(c * PIECE, PIECE), pl.ds(0, length)]
        return pltpu.make_async_remote_copy(
            src_ref=src,
            dst_ref=dst,
            send_sem=ar_send.at[s, h, c],
            recv_sem=ar_recv.at[s, h, c],
            device_id={"subj": peer},
            device_id_type=MESH,
        )

    def finish(s, c):
        for h in range(2):
            step(s, h, c).wait_recv()
            if s < bits:
                peer, kept, sent, length = plans[h][s]
                here = pl.ds(c * PIECE, PIECE)
                core = pl.ds(BLOCK + c * PIECE, PIECE)
                new = got[s, h, here, pl.ds(0, length), :]
                if s == 0:
                    old = iw[core, ds(kept, length), :]
                else:
                    above = plans[h][s - 1][1]
                    old = part[s - 1, h, here, ds(kept - above, length), :]
                if s < bits - 1:
                    part[s, h, here, pl.ds(0, length), :] = old + new
                else:
                    jw[core, ds(kept, length), :] = (old + new) / members
            if s + 1 < stages:
                step(s + 1, h, c).start()

    def halo(which, way, recv, what):
        core = 0 if way == 0 else planes - BLOCK
        there = planes + BLOCK if way == 0 else 0
        wide = iw if which == 0 else jw
        if which == 0:
            src = x.at[0, pl.ds(core, BLOCK)]
        else:
            src = jw.at[pl.ds(core + BLOCK, BLOCK)]
        peer = gz - 1 if way == 0 else gz + 1
        can_send = has_low if way == 0 else has_high
        can_take = has_high if way == 0 else has_low
        copy = pltpu.make_async_remote_copy(
            src_ref=src,
            dst_ref=wide.at[pl.ds(there, BLOCK)],
            send_sem=halo_send.at[which, way],
            recv_sem=halo_recv.at[which, way],
            device_id={"gz": lax.rem(peer + size, size)},
            device_id_type=MESH,
        )

        @pl.when(can_take if recv else can_send)
        def _():
            if what == "start":
                copy.start()
            elif recv:
                copy.wait_recv()
            else:
                copy.wait_send()

    edge = BLOCK // PIECE
    ahead = 3

    def first(pos):
        if pos < pieces:
            for h in range(2):
                step(0, h, pos).start()

    for pos in range(ahead):
        first(pos)
    halo(0, 0, 0, "start")
    halo(0, 1, 0, "start")

    nothing = jnp.zeros((BLOCK, rows, cols), F32)

    @pl.when(jnp.logical_not(has_low))
    def _():
        iw[pl.ds(0, BLOCK)] = nothing
        jw[pl.ds(0, BLOCK)] = nothing

    @pl.when(jnp.logical_not(has_high))
    def _():
        iw[pl.ds(planes + BLOCK, BLOCK)] = nothing
        jw[pl.ds(planes + BLOCK, BLOCK)] = nothing

    loss[...] = jnp.zeros_like(loss)
    blocks = chunks + 1
    last = stages - 1
    events = sorted((pos + s, -s, pos) for s in range(stages) for pos in range(pieces))

    def need(slot):
        return last + min(pieces, edge * (slot + 2)) - 1

    def place(key):
        if key < need(0):
            return 0, key * blocks // need(0)
        slot = min(t for t in range(blocks) if need(t) >= key)
        return (1, slot) if key == need(slot) else (2, slot - 1)

    def serve(kind, slot):
        for key, s, pos in events:
            if place(key) == (kind, slot):
                finish(-s, pos)
                if s == 0:
                    first(pos + ahead)
                if -s == stages - 1 and pos == edge - 1:
                    halo(1, 0, 0, "start")
                if -s == stages - 1 and pos == pieces - 1:
                    halo(1, 1, 0, "start")

    def block_of(i):
        return jnp.where(i < chunks, i + 1, 0)

    for load in loads:
        load.wait()

    def moving_part(i, _):
        for slot in range(blocks):

            @pl.when(i == slot)
            def _(slot=slot):
                serve(0, slot)
                if slot == chunks - 1:
                    halo(0, 0, 1, "wait")
                if slot == chunks:
                    halo(0, 1, 1, "wait")

        box_block(block_of(i), 0, 2, iw, jw, xy, t_ref, by, bx)
        return 0

    lax.fori_loop(0, blocks, moving_part, 0)

    def raw_copy(b):
        at = pl.ds(b * BLOCK, BLOCK)
        return pltpu.make_async_copy(r_ref.at[:, at], raw.at[:, at], put_sem.at[b])

    def target_part(i, _):
        for slot in range(blocks):

            @pl.when(i == slot)
            def _(slot=slot):
                serve(1, slot)
                if slot == chunks - 1:
                    halo(1, 0, 1, "wait")
                if slot == chunks:
                    halo(1, 1, 1, "wait")

        b = block_of(i)
        box_block(b, 2, 3, iw, jw, xy, t_ref, by, bx)

        for slot in range(chunks - 1):

            @pl.when(i == slot)
            def _(slot=slot):
                serve(2, slot)

        force_block(b, z_first, depth, planes, iw, jw, r_ref, t_ref, loss)
        raw_copy(b).start()
        return 0

    lax.fori_loop(0, blocks, target_part, 0)
    whole = pltpu.make_async_copy(jw.at[pl.ds(BLOCK, planes)], template, put_sem.at[blocks])
    whole.start()

    total = jnp.zeros((8, 128), F32)
    for row in range(0, rows, 8):
        for lane in range(0, cols, 128):
            total = total + loss[pl.ds(row, 8), pl.ds(lane, 128)]
    loss_all[gz] = total

    def share(d):
        return pltpu.make_async_remote_copy(
            src_ref=loss_all.at[gz],
            dst_ref=loss_all.at[gz],
            send_sem=loss_send.at[d],
            recv_sem=loss_recv.at[d],
            device_id={"gz": lax.rem(gz + d, size)},
            device_id_type=MESH,
        )

    for d in range(1, size):
        share(d).start()

    for d in range(1, size):
        share(d).wait_recv()
    sims = loss_all[0]
    for k in range(1, size):
        sims = sims + loss_all[k]
    loss_out[0] = -jnp.sum(sims) / float(depth * rows * cols)

    for b in range(blocks):
        raw_copy(b).wait()
    whole.wait()
    for d in range(1, size):
        share(d).wait_send()
    for s in range(stages):
        for h in range(2):
            for c in range(pieces):
                step(s, h, c).wait_send()
    for which in range(2):
        for way in range(2):
            halo(which, way, 0, "wait")


def blur_kernel(weights, raw, mean, gy, gx, out, template, r_ref, yx, out_v, mean_v, load_sem, put_sem):
    planes, rows, cols = out.shape[2:]
    blocks = raw.shape[1] // BLOCK

    def load(b):
        at = pl.ds(b * BLOCK, BLOCK)
        return pltpu.make_async_copy(raw.at[:, at], r_ref.at[:, at], load_sem.at[b])

    for b in range(blocks):
        load(b).start()
    mean_in = pltpu.make_async_copy(mean, mean_v, load_sem.at[blocks])
    mean_out = pltpu.make_async_copy(mean_v, template, put_sem.at[planes // GROUP])
    mean_in.start()
    load(0).wait()

    def put(k, base, value):
        out_v[k, pl.ds(base, GROUP)] = jnp.reshape(value, (GROUP, rows, cols))

    def put_copy(g):
        at = pl.ds(g * GROUP, GROUP)
        return pltpu.make_async_copy(out_v.at[:, at], out.at[0, :, at], put_sem.at[g])

    def blur(g, _):
        @pl.when(lax.rem(g, BLOCK // GROUP) == 0)
        def _():
            load(g // (BLOCK // GROUP) + 1).wait()

        @pl.when(g == planes // GROUP - 4)
        def _():
            mean_in.wait()
            mean_out.start()

        blur_block(g, weights, r_ref, yx, gy, gx, put)
        put_copy(g).start()
        return 0

    lax.fori_loop(0, planes // GROUP, blur, 0)
    for g in range(planes // GROUP):
        put_copy(g).wait()
    mean_out.wait()


def on_device(warped):
    planes, rows, cols = warped.shape[1:]
    members, size = lax.axis_size("subj"), lax.axis_size("gz")
    bits = members.bit_length() - 1
    assert members == 1 << bits and bits > 1 and planes % BLOCK == 0
    by, bx, gy, gx, weights = bands(rows, cols)
    chunks, pieces = planes // BLOCK, planes // PIECE
    stages = 2 * bits - 1
    grows = GROUP * rows
    vmem = pl.BlockSpec(memory_space=pltpu.VMEM)
    anywhere = pl.BlockSpec(memory_space=pl.ANY)
    cells = planes * rows * cols
    dma = pltpu.SemaphoreType.DMA
    raw_shape = (3, planes + BLOCK, rows, cols)
    raw, mean, loss = pl.pallas_call(
        functools.partial(kernel, (members, size)),
        out_shape=(
            jax.ShapeDtypeStruct(raw_shape, F32),
            jax.ShapeDtypeStruct((planes, rows, cols), F32),
            jax.ShapeDtypeStruct((1,), F32),
        ),
        in_specs=[anywhere] + [vmem] * 2,
        out_specs=(anywhere, anywhere, pl.BlockSpec(memory_space=pltpu.SMEM)),
        scratch_shapes=[
            pltpu.VMEM((planes + 2 * BLOCK, rows, cols), F32),
            pltpu.VMEM((planes + 2 * BLOCK, rows, cols), F32),
            pltpu.VMEM((bits - 1, 2, planes, rows // 4, cols), F32),
            pltpu.VMEM((bits, 2, planes, rows // 4, cols), F32),
            pltpu.VMEM(raw_shape, F32),
            pltpu.VMEM((3, BLOCK // GROUP, 3 * grows, cols), BF16),
            pltpu.VMEM((5, (planes + BLOCK) * rows, cols), F32),
            pltpu.VMEM((rows, cols), F32),
            pltpu.VMEM((size, 8, 128), F32),
            dma((chunks,)),
            dma((stages, 2, pieces)),
            dma((stages, 2, pieces)),
            dma((2, 2)),
            dma((2, 2)),
            dma((size,)),
            dma((size,)),
            dma((chunks + 2,)),
        ],
        compiler_params=pltpu.CompilerParams(
            collective_id=0, has_side_effects=True, vmem_limit_bytes=60 * 1024 * 1024
        ),
        cost_estimate=pl.CostEstimate(
            flops=200 * cells, bytes_accessed=20 * cells, transcendentals=0
        ),
    )(warped, by, bx)
    force, template = pl.pallas_call(
        functools.partial(blur_kernel, weights),
        out_shape=(
            jax.ShapeDtypeStruct((1, 3, planes, rows, cols), F32),
            jax.ShapeDtypeStruct((planes, rows, cols), F32),
        ),
        in_specs=[anywhere, anywhere, vmem, vmem],
        out_specs=(anywhere, anywhere),
        scratch_shapes=[
            pltpu.VMEM(raw_shape, F32),
            pltpu.VMEM((3, grows, 3 * cols), BF16),
            pltpu.VMEM((3, planes, rows, cols), F32),
            pltpu.VMEM((planes, rows, cols), F32),
            dma((chunks + 2,)),
            dma((planes // GROUP + 1,)),
        ],
        compiler_params=pltpu.CompilerParams(vmem_limit_bytes=60 * 1024 * 1024),
        cost_estimate=pl.CostEstimate(
            flops=100 * cells, bytes_accessed=32 * cells, transcendentals=0
        ),
    )(raw, mean, gy, gx)
    return (force, template, loss)


def solution(mesh):
    placed = (P("subj", "gz", None, None),)
    return jax.shard_map(
        on_device,
        mesh=mesh,
        in_specs=placed,
        out_specs=(P("subj", None, "gz", None, None), P("gz", None, None), P("subj")),
        check_vma=False,
    )
```

```python
import functools
import math

import jax
import jax.numpy as jnp
import ml_dtypes
import numpy as np
from jax import lax
from jax.experimental import pallas as pl
from jax.experimental.pallas import tpu as pltpu
from jax.sharding import PartitionSpec as P

BOX_R = 4
GAUSS_R = 3
EPS = 1e-05
BLOCK = 8
GROUP = 4
STRIP = 16
PIECE = 8
F32 = jnp.float32
BF16 = jnp.bfloat16
MESH = pl.DeviceIdType.MESH


def bands(rows, cols):
    bumps = np.array([math.exp(-(k * k) / 8.0) for k in range(-GAUSS_R, GAUSS_R + 1)])
    bumps = bumps / bumps.sum()

    def band(n, weights, radius):
        out = np.zeros((n, n), np.float32)
        for k in range(-radius, radius + 1):
            out += np.diag(np.full(n - abs(k), weights[k + radius], np.float32), k)
        return out

    def high_low(m):
        high = m.astype(ml_dtypes.bfloat16)
        low = (m - high.astype(np.float32)).astype(ml_dtypes.bfloat16)
        return high, low

    ones = np.ones(2 * BOX_R + 1)
    eye = np.eye(GROUP, dtype=np.float32)
    box_y = np.kron(eye, band(rows, ones, BOX_R)).astype(ml_dtypes.bfloat16)
    box_x = band(cols, ones, BOX_R).astype(ml_dtypes.bfloat16)
    gy_high, gy_low = high_low(np.kron(eye, band(rows, bumps, GAUSS_R)))
    gx_high, gx_low = high_low(band(cols, bumps, GAUSS_R))
    return (
        np.concatenate([box_y] * 3, axis=1),
        np.concatenate([box_x] * 3, axis=0),
        np.concatenate([gy_high, gy_high, gy_low], axis=1),
        np.concatenate([gx_high, gx_high, gx_low], axis=0),
        [float(b) for b in bumps[GAUSS_R:]],
    )


def split3(v):
    a = v.astype(BF16)
    r = v - a.astype(F32)
    b = r.astype(BF16)
    c = (r - b.astype(F32)).astype(BF16)
    return a, b, c


def split2(v):
    a = v.astype(BF16)
    return a, (v - a.astype(F32)).astype(BF16)


def windows(planes):
    n = BLOCK
    span = 2 * BOX_R + 1
    head = [None] * (n + 1)
    acc = planes[n - 1]
    head[n - 1] = acc
    for i in range(n - 2, -1, -1):
        acc = acc + planes[i]
        head[i] = acc
    out = []
    tail = None
    for i in range(n):
        tail = planes[n + i] if tail is None else tail + planes[n + i]
        out.append(head[i] + tail)
    assert span == n + 1
    return out


def box_block(b, first, count, iw, jw, xy, t_ref, by, bx):
    rows, cols = iw.shape[1], iw.shape[2]
    base = b * BLOCK
    grows = GROUP * rows
    span = BLOCK + 2 * BOX_R

    def strips(v):
        for row in range(0, rows, STRIP):
            for lane in range(0, cols, 128):
                at = (pl.ds(row, STRIP), pl.ds(lane, 128))
                if v in (0, 1, 4):
                    iv = [iw[(base + k,) + at] for k in range(span)]
                if v > 1:
                    jv = [jw[(base + k,) + at] for k in range(span)]
                if v == 0:
                    vol = iv
                elif v == 1:
                    vol = [a * a for a in iv]
                elif v == 2:
                    vol = jv
                elif v == 3:
                    vol = [a * a for a in jv]
                else:
                    vol = [a * c for a, c in zip(iv, jv)]
                for w, total in enumerate(windows(vol)):
                    g, u = w // GROUP, w % GROUP
                    for k, piece in enumerate(split3(total)):
                        low = k * grows + u * rows + row
                        xy[v - first, g, pl.ds(low, STRIP), pl.ds(lane, 128)] = piece

    def products(v, g):
        at = pl.multiple_of(b * BLOCK * rows + g * grows, grows)
        ys = jnp.dot(by[...], xy[v - first, g], preferred_element_type=F32)
        xs = jnp.concatenate(split3(ys), axis=1)
        t_ref[v, pl.ds(at, grows), :] = jnp.dot(xs, bx[...], preferred_element_type=F32)

    strips(first)
    for v in range(first, first + count):
        if v + 1 < first + count:
            strips(v + 1)
        for g in range(BLOCK // GROUP):
            products(v, g)


def force_block(b, z_first, depth, planes, iw, jw, r_ref, t_ref, loss):
    rows, cols = iw.shape[1], iw.shape[2]
    scale = 1.0 / float((2 * BOX_R + 1) ** 3)

    def plane(u, _):
        c = b * BLOCK + u
        at = pl.multiple_of(c * rows, rows)
        m = [t_ref[v, pl.ds(at, rows), :] * scale for v in range(5)]
        mi, mj = m[0], m[2]
        var_i = m[1] - mi * mi
        var_j = m[3] - mj * mj
        cc = m[4] - mi * mj
        moving = iw[c + BOX_R]
        target = jw[c + BOX_R]
        q = cc / (var_i * var_j + EPS)
        core = c - BOX_R
        z = z_first + core
        owned = jnp.logical_and(core >= 0, core < planes)
        loss[...] += jnp.where(owned, cc * q, 0.0)
        factor = q * ((target - mj) - cc / (var_i + EPS) * (moving - mi))
        inside = jnp.logical_and(z >= 0, z < depth)
        factor = jnp.where(inside, factor, 0.0)
        row_id = lax.broadcasted_iota(jnp.int32, moving.shape, 0)
        col_id = lax.broadcasted_iota(jnp.int32, moving.shape, 1)
        dz = iw[c + BOX_R + 1] - iw[c + BOX_R - 1]
        dy = jnp.where(row_id == rows - 1, 0.0, pltpu.roll(moving, rows - 1, 0)) - jnp.where(
            row_id == 0, 0.0, pltpu.roll(moving, 1, 0)
        )
        dx = jnp.where(col_id == cols - 1, 0.0, pltpu.roll(moving, cols - 1, 1)) - jnp.where(
            col_id == 0, 0.0, pltpu.roll(moving, 1, 1)
        )
        r_ref[0, c] = factor * dz
        r_ref[1, c] = factor * dy
        r_ref[2, c] = factor * dx
        return 0

    lax.fori_loop(0, BLOCK, plane, 0)


def blur_block(b, weights, r_ref, yx, gy, gx, put):
    rows, cols = r_ref.shape[2], r_ref.shape[3]
    base = b * GROUP

    def strips(k):
        for row in range(0, rows, STRIP):
            for lane in range(0, cols, 128):
                v = [
                    r_ref[k, base + BOX_R - GAUSS_R + j, pl.ds(row, STRIP), pl.ds(lane, 128)]
                    for j in range(GROUP + 2 * GAUSS_R)
                ]
                for u in range(GROUP):
                    mid = u + GAUSS_R
                    total = weights[0] * v[mid]
                    for o in range(1, GAUSS_R + 1):
                        total = total + weights[o] * (v[mid - o] + v[mid + o])
                    high, low = split2(total)
                    at = u * rows + row
                    yx[k, pl.ds(at, STRIP), pl.ds(lane, 128)] = high
                    yx[k, pl.ds(at, STRIP), pl.ds(cols + lane, 128)] = low
                    yx[k, pl.ds(at, STRIP), pl.ds(2 * cols + lane, 128)] = high

    def products(k):
        xs = jnp.dot(yx[k], gx[...], preferred_element_type=F32)
        high, low = split2(xs)
        both = jnp.concatenate([high, low, high], axis=0)
        put(k, base, jnp.dot(gy[...], both, preferred_element_type=F32))

    strips(0)
    for k in range(3):
        if k < 2:
            strips(k + 1)
        products(k)


def kernel(
    shape, x, by, bx, raw, template, loss_out,
    iw, jw, part, got, r_ref, xy, t_ref, loss, loss_all,
    load_sem, ar_send, ar_recv, halo_send, halo_recv, loss_send, loss_recv, put_sem,
):
    members, size = shape
    planes, rows, cols = x.shape[1:]
    bits = members.bit_length() - 1
    chunks = planes // BLOCK
    pieces = planes // PIECE
    stages = 2 * bits - 1
    me = lax.axis_index("subj")
    gz = lax.axis_index("gz")
    z_first, depth = gz * planes, planes * size
    has_low, has_high = gz > 0, gz < size - 1

    def flip(bit):
        mine = (me // (1 << bit)) % 2
        return mine, me + (1 - 2 * mine) * (1 << bit)

    barrier = pltpu.get_barrier_semaphore()
    for bit in range(bits):
        pl.semaphore_signal(barrier, inc=1, device_id={"subj": flip(bit)[1]}, device_id_type=MESH)
    for d in range(1, size):
        peer = lax.rem(gz + d, size)
        pl.semaphore_signal(barrier, inc=1, device_id={"gz": peer}, device_id_type=MESH)

    loads = [
        pltpu.make_async_copy(
            x.at[0, pl.ds(c * BLOCK, BLOCK)], iw.at[pl.ds((c + 1) * BLOCK, BLOCK)], load_sem.at[c]
        )
        for c in range(chunks)
    ]
    for load in loads:
        load.start()
    pl.semaphore_wait(barrier, bits + size - 1)

    half = rows // 2
    plans = []
    for h in range(2):
        order = list(range(bits)) if h == 0 else list(range(bits))[::-1]
        at, length, levels = h * half, half, []
        for bit in order[:-1]:
            mine, peer = flip(bit)
            length //= 2
            kept = at + mine * length
            levels.append((peer, kept, at + (1 - mine) * length, length))
            at = kept
        levels.append((flip(order[-1])[1], at, at, length))
        plans.append(levels)

    def ds(at, length):
        return pl.ds(pl.multiple_of(at, length), length)

    def step(s, h, c):
        deep = s if s < bits else stages - 1 - s
        peer, kept, sent, length = plans[h][deep]
        wide = pl.ds(BLOCK + c * PIECE, PIECE)
        if s >= bits:
            src = jw.at[wide, ds(kept, length)]
            dst = src
        else:
            if s == 0:
                src = x.at[0, pl.ds(c * PIECE, PIECE), ds(sent, length)]
            else:
                above = plans[h][s - 1][1]
                src = part.at[s - 1, h, pl.ds(c * PIECE, PIECE), ds(sent - above, length)]
            dst = got.at[s, h, pl.ds(c * PIECE, PIECE), pl.ds(0, length)]
        return pltpu.make_async_remote_copy(
            src_ref=src,
            dst_ref=dst,
            send_sem=ar_send.at[s, h, c],
            recv_sem=ar_recv.at[s, h, c],
            device_id={"subj": peer},
            device_id_type=MESH,
        )

    def finish(s, c):
        for h in range(2):
            step(s, h, c).wait_recv()
            if s < bits:
                peer, kept, sent, length = plans[h][s]
                here = pl.ds(c * PIECE, PIECE)
                core = pl.ds(BLOCK + c * PIECE, PIECE)
                new = got[s, h, here, pl.ds(0, length), :]
                if s == 0:
                    old = iw[core, ds(kept, length), :]
                else:
                    above = plans[h][s - 1][1]
                    old = part[s - 1, h, here, ds(kept - above, length), :]
                if s < bits - 1:
                    part[s, h, here, pl.ds(0, length), :] = old + new
                else:
                    jw[core, ds(kept, length), :] = (old + new) / members
            if s + 1 < stages:
                step(s + 1, h, c).start()

    def halo(which, way, recv, what):
        core = 0 if way == 0 else planes - BLOCK
        there = planes + BLOCK if way == 0 else 0
        wide = iw if which == 0 else jw
        if which == 0:
            src = x.at[0, pl.ds(core, BLOCK)]
        else:
            src = jw.at[pl.ds(core + BLOCK, BLOCK)]
        peer = gz - 1 if way == 0 else gz + 1
        can_send = has_low if way == 0 else has_high
        can_take = has_high if way == 0 else has_low
        copy = pltpu.make_async_remote_copy(
            src_ref=src,
            dst_ref=wide.at[pl.ds(there, BLOCK)],
            send_sem=halo_send.at[which, way],
            recv_sem=halo_recv.at[which, way],
            device_id={"gz": lax.rem(peer + size, size)},
            device_id_type=MESH,
        )

        @pl.when(can_take if recv else can_send)
        def _():
            if what == "start":
                copy.start()
            elif recv:
                copy.wait_recv()
            else:
                copy.wait_send()

    edge = BLOCK // PIECE
    ahead = 2

    def first(pos):
        if pos < pieces:
            for h in range(2):
                step(0, h, pos).start()

    for pos in range(ahead):
        first(pos)
    halo(0, 0, 0, "start")
    halo(0, 1, 0, "start")

    nothing = jnp.zeros((BLOCK, rows, cols), F32)

    @pl.when(jnp.logical_not(has_low))
    def _():
        iw[pl.ds(0, BLOCK)] = nothing
        jw[pl.ds(0, BLOCK)] = nothing

    @pl.when(jnp.logical_not(has_high))
    def _():
        iw[pl.ds(planes + BLOCK, BLOCK)] = nothing
        jw[pl.ds(planes + BLOCK, BLOCK)] = nothing

    loss[...] = jnp.zeros_like(loss)
    blocks = chunks + 1
    last = 3 * (stages - 1)
    events = sorted((2 * pos + 3 * s, -s, pos) for s in range(stages) for pos in range(pieces))

    def need(slot):
        return last + 2 * (min(pieces, edge * (slot + 2)) - 1)

    def place(event):
        key = event[0]
        if key <= need(0):
            index = events.index(event)
            return (0, index) if index < blocks else (1, 0)
        slot = min(t for t in range(blocks) if need(t) >= key)
        return (1, slot) if key == need(slot) else (2, slot - 1)

    def serve(kind, slot):
        for event in events:
            key, s, pos = event
            if place(event) == (kind, slot):
                finish(-s, pos)
                if s == 0:
                    first(pos + ahead)
                if -s == stages - 1 and pos == edge - 1:
                    halo(1, 0, 0, "start")
                if -s == stages - 1 and pos == pieces - 1:
                    halo(1, 1, 0, "start")

    def block_of(i):
        return jnp.where(i < chunks, i + 1, 0)

    for load in loads:
        load.wait()

    def moving_part(i, _):
        for slot in range(blocks):

            @pl.when(i == slot)
            def _(slot=slot):
                serve(0, slot)
                if slot == chunks - 1:
                    halo(0, 0, 1, "wait")
                if slot == chunks:
                    halo(0, 1, 1, "wait")

        box_block(block_of(i), 0, 2, iw, jw, xy, t_ref, by, bx)
        return 0

    lax.fori_loop(0, blocks, moving_part, 0)

    def raw_copy(b):
        at = pl.ds(b * BLOCK, BLOCK)
        return pltpu.make_async_copy(r_ref.at[:, at], raw.at[:, at], put_sem.at[b])

    def target_part(i, _):
        for slot in range(blocks):

            @pl.when(i == slot)
            def _(slot=slot):
                serve(1, slot)
                if slot == chunks - 1:
                    halo(1, 0, 1, "wait")
                if slot == chunks:
                    halo(1, 1, 1, "wait")

        b = block_of(i)
        box_block(b, 2, 3, iw, jw, xy, t_ref, by, bx)

        for slot in range(chunks - 1):

            @pl.when(i == slot)
            def _(slot=slot):
                serve(2, slot)

        force_block(b, z_first, depth, planes, iw, jw, r_ref, t_ref, loss)
        raw_copy(b).start()
        return 0

    lax.fori_loop(0, blocks, target_part, 0)
    whole = pltpu.make_async_copy(jw.at[pl.ds(BLOCK, planes)], template, put_sem.at[blocks])
    whole.start()

    total = jnp.zeros((8, 128), F32)
    for row in range(0, rows, 8):
        for lane in range(0, cols, 128):
            total = total + loss[pl.ds(row, 8), pl.ds(lane, 128)]
    loss_all[gz] = total

    def share(d):
        return pltpu.make_async_remote_copy(
            src_ref=loss_all.at[gz],
            dst_ref=loss_all.at[gz],
            send_sem=loss_send.at[d],
            recv_sem=loss_recv.at[d],
            device_id={"gz": lax.rem(gz + d, size)},
            device_id_type=MESH,
        )

    for d in range(1, size):
        share(d).start()

    for d in range(1, size):
        share(d).wait_recv()
    sims = loss_all[0]
    for k in range(1, size):
        sims = sims + loss_all[k]
    loss_out[0] = -jnp.sum(sims) / float(depth * rows * cols)

    for b in range(blocks):
        raw_copy(b).wait()
    whole.wait()
    for d in range(1, size):
        share(d).wait_send()
    for s in range(stages):
        for h in range(2):
            for c in range(pieces):
                step(s, h, c).wait_send()
    for which in range(2):
        for way in range(2):
            halo(which, way, 0, "wait")


def blur_kernel(weights, raw, mean, gy, gx, out, template, r_ref, yx, out_v, mean_v, load_sem, put_sem):
    planes, rows, cols = out.shape[2:]
    blocks = raw.shape[1] // BLOCK

    def load(b):
        at = pl.ds(b * BLOCK, BLOCK)
        return pltpu.make_async_copy(raw.at[:, at], r_ref.at[:, at], load_sem.at[b])

    for b in range(blocks):
        load(b).start()
    mean_in = pltpu.make_async_copy(mean, mean_v, load_sem.at[blocks])
    mean_out = pltpu.make_async_copy(mean_v, template, put_sem.at[planes // GROUP])
    mean_in.start()
    load(0).wait()

    def put(k, base, value):
        out_v[k, pl.ds(base, GROUP)] = jnp.reshape(value, (GROUP, rows, cols))

    def put_copy(g):
        at = pl.ds(g * GROUP, GROUP)
        return pltpu.make_async_copy(out_v.at[:, at], out.at[0, :, at], put_sem.at[g])

    def blur(g, _):
        @pl.when(lax.rem(g, BLOCK // GROUP) == 0)
        def _():
            load(g // (BLOCK // GROUP) + 1).wait()

        @pl.when(g == planes // GROUP - 4)
        def _():
            mean_in.wait()
            mean_out.start()

        blur_block(g, weights, r_ref, yx, gy, gx, put)
        put_copy(g).start()
        return 0

    lax.fori_loop(0, planes // GROUP, blur, 0)
    for g in range(planes // GROUP):
        put_copy(g).wait()
    mean_out.wait()


def on_device(warped):
    planes, rows, cols = warped.shape[1:]
    members, size = lax.axis_size("subj"), lax.axis_size("gz")
    bits = members.bit_length() - 1
    assert members == 1 << bits and bits > 1 and planes % BLOCK == 0
    by, bx, gy, gx, weights = bands(rows, cols)
    chunks, pieces = planes // BLOCK, planes // PIECE
    stages = 2 * bits - 1
    grows = GROUP * rows
    vmem = pl.BlockSpec(memory_space=pltpu.VMEM)
    anywhere = pl.BlockSpec(memory_space=pl.ANY)
    cells = planes * rows * cols
    dma = pltpu.SemaphoreType.DMA
    raw_shape = (3, planes + BLOCK, rows, cols)
    raw, mean, loss = pl.pallas_call(
        functools.partial(kernel, (members, size)),
        out_shape=(
            jax.ShapeDtypeStruct(raw_shape, F32),
            jax.ShapeDtypeStruct((planes, rows, cols), F32),
            jax.ShapeDtypeStruct((1,), F32),
        ),
        in_specs=[anywhere] + [vmem] * 2,
        out_specs=(anywhere, anywhere, pl.BlockSpec(memory_space=pltpu.SMEM)),
        scratch_shapes=[
            pltpu.VMEM((planes + 2 * BLOCK, rows, cols), F32),
            pltpu.VMEM((planes + 2 * BLOCK, rows, cols), F32),
            pltpu.VMEM((bits - 1, 2, planes, rows // 4, cols), F32),
            pltpu.VMEM((bits, 2, planes, rows // 4, cols), F32),
            pltpu.VMEM(raw_shape, F32),
            pltpu.VMEM((3, BLOCK // GROUP, 3 * grows, cols), BF16),
            pltpu.VMEM((5, (planes + BLOCK) * rows, cols), F32),
            pltpu.VMEM((rows, cols), F32),
            pltpu.VMEM((size, 8, 128), F32),
            dma((chunks,)),
            dma((stages, 2, pieces)),
            dma((stages, 2, pieces)),
            dma((2, 2)),
            dma((2, 2)),
            dma((size,)),
            dma((size,)),
            dma((chunks + 2,)),
        ],
        compiler_params=pltpu.CompilerParams(
            collective_id=0, has_side_effects=True, vmem_limit_bytes=60 * 1024 * 1024
        ),
        cost_estimate=pl.CostEstimate(
            flops=200 * cells, bytes_accessed=20 * cells, transcendentals=0
        ),
    )(warped, by, bx)
    force, template = pl.pallas_call(
        functools.partial(blur_kernel, weights),
        out_shape=(
            jax.ShapeDtypeStruct((1, 3, planes, rows, cols), F32),
            jax.ShapeDtypeStruct((planes, rows, cols), F32),
        ),
        in_specs=[anywhere, anywhere, vmem, vmem],
        out_specs=(anywhere, anywhere),
        scratch_shapes=[
            pltpu.VMEM(raw_shape, F32),
            pltpu.VMEM((3, grows, 3 * cols), BF16),
            pltpu.VMEM((3, planes, rows, cols), F32),
            pltpu.VMEM((planes, rows, cols), F32),
            dma((chunks + 2,)),
            dma((planes // GROUP + 1,)),
        ],
        compiler_params=pltpu.CompilerParams(vmem_limit_bytes=60 * 1024 * 1024),
        cost_estimate=pl.CostEstimate(
            flops=100 * cells, bytes_accessed=32 * cells, transcendentals=0
        ),
    )(raw, mean, gy, gx)
    return (force, template, loss)


def solution(mesh):
    placed = (P("subj", "gz", None, None),)
    return jax.shard_map(
        on_device,
        mesh=mesh,
        in_specs=placed,
        out_specs=(P("subj", None, "gz", None, None), P("gz", None, None), P("subj")),
        check_vma=False,
    )
```
